128 devices in a mesh: fsdp: 16 (over x, z_hi, core), replica: 8 (over y, z_lo).
Axes of the slice: x: 4, y: 4, z: 4 (z_hi: 2, z_lo: 2; z = z_hi * 2 + z_lo), core: 2. Of those that a mesh axis runs over, the one named last changes fastest.
Arguments:
- tokens: bfloat16 [131072, 4096], P(('fsdp', 'replica')), may hold values from -180 to 180
- norm_gain: float32 [4096], replicated, may hold values from 0.1 to 1.9
- key_weight: bfloat16 [4096, 512], P('fsdp'), may hold values from -0.09375 to 0.09375
- value_weight: bfloat16 [4096, 512], P('fsdp'), may hold values from -0.09375 to 0.09375
- key_cotangent: bfloat16 [131072, 512], P(('fsdp', 'replica')), may hold values from -6 to 6
- value_cotangent: bfloat16 [131072, 512], P(('fsdp', 'replica')), may hold values from -6 to 6
Outputs:
- rotated_keys: bfloat16 [131072, 512], P(('fsdp', 'replica'))
- value_rows: bfloat16 [131072, 512], P(('fsdp', 'replica'))
- input_grad: bfloat16 [131072, 4096], P(('fsdp', 'replica'))
- key_weight_grad: float32 [4096, 512], P('fsdp')
- value_weight_grad: float32 [4096, 512], P('fsdp')
- gain_grad: float32 [4096], replicated
The draws below stay inside these ranges and needn't reach their ends.
All inputs are finite; a program needn't handle non-finite values.
Results may differ from the reference program's by a relative error of at most 0.005.
Values may be sent and summed in bfloat16 or wider, within the bound.
No kernel may reach another device: no remote copies, remote signals or barrier semaphores. Data moves between devices by JAX's collectives and lax.ppermute only.
A program may use at most 192 MiB of HBM per device.

```python
import math
import jax
import jax.numpy as jnp
from jax import lax

D = 4096
HEAD = 128
SEQ = 1024
KV = 512
TOKENS = 131072


def draw_tokens(key, part):
    first, second, third = jax.random.split(key, 3)
    base = jnp.clip(jax.random.normal(first, (TOKENS, D), jnp.float32), -6.0, 6.0)
    row_scale = jnp.exp(jax.random.uniform(second, (TOKENS, 1), jnp.float32, 0.0, math.log(10.0)))
    col_scale = jnp.exp(jax.random.uniform(third, (1, D), jnp.float32, math.log(0.3), math.log(3.0)))
    return (base * row_scale * col_scale).astype(jnp.bfloat16)


def steps_of(key, shape, shards, low, top_value):
    level = 1.0
    for position, blocks in shards:
        draws = jax.random.uniform(jax.random.fold_in(jax.random.fold_in(key, 6), position), (blocks,), jnp.float32, low / len(shards), top_value / len(shards))
        level = level * jnp.repeat(jnp.exp(draws), shape[position] // blocks).reshape((-1,) + (1,) * (len(shape) - 1 - position))
    return level


def centred(rng, extent, spread, reach, shards=(), held_as=jnp.bfloat16):
    loudness = steps_of(rng, extent, shards, -0.22, 0.18) if shards else 1.0
    result = jax.random.normal(rng, extent, jnp.float32) * spread * loudness
    return jnp.minimum(jnp.maximum(result, -reach), reach).astype(held_as)


def setup_inputs(seed: int = 0) -> dict:
    seeds = jax.random.split(jax.random.key(seed), 7)
    tokens = draw_tokens(jax.random.fold_in(seeds[6], 71), 0)
    norm_gain = jnp.clip(1.0 + 0.18 * jax.random.normal(seeds[1], (D,), jnp.float32), 0.1, 1.9)
    key_weight = centred(seeds[2], (D, KV), D ** -0.5, 0.09375, ((0, 16),))
    value_weight = centred(seeds[3], (D, KV), D ** -0.5, 0.09375, ((0, 16),))
    key_cotangent = centred(seeds[4], (TOKENS, KV), 1.0, 6.0, ((0, 128),))
    value_cotangent = centred(seeds[5], (TOKENS, KV), 1.0, 6.0, ((0, 128),))
    return dict(tokens=tokens, norm_gain=norm_gain, key_weight=key_weight, value_weight=value_weight, key_cotangent=key_cotangent, value_cotangent=value_cotangent)


def tables(length):
    half = HEAD // 2
    places = jnp.arange(length, dtype=jnp.float32)
    inverse = jnp.exp(-(2.0 * jnp.arange(half, dtype=jnp.float32) / HEAD) * math.log(500000.0))
    angles = places[:, None] * inverse[None, :]
    return (jnp.cos(angles)[:, None, :], jnp.sin(angles)[:, None, :])

def rotate(values, cosine, sine, direction):
    length = values.shape[0]
    half = HEAD // 2
    heads = values.reshape(length, -1, HEAD)
    first = heads[..., :half]
    second = heads[..., half:]
    out_first = first * cosine - direction * second * sine
    out_second = second * cosine + direction * first * sine
    return jnp.concatenate([out_first, out_second], axis=2).reshape(length, -1)

def sequence_pass(rows, key_cot, value_cot, gain, key_w, value_w, cosine, sine):
    floats = rows.astype(jnp.float32)
    inv_scale = lax.rsqrt(lax.optimization_barrier(jnp.mean(floats * floats, axis=1, keepdims=True)) + 1e-05)
    normed = (floats * inv_scale * gain[None, :]).astype(jnp.bfloat16)
    key_pre = jnp.dot(normed, key_w, preferred_element_type=jnp.float32)
    value_pre = jnp.dot(normed, value_w, preferred_element_type=jnp.float32)
    keys_out = rotate(key_pre, cosine, sine, 1.0).astype(jnp.bfloat16)
    values_out = value_pre.astype(jnp.bfloat16)
    key_back = rotate(key_cot.astype(jnp.float32), cosine, sine, -1.0).astype(jnp.bfloat16)
    contract = (((1,), (1,)), ((), ()))
    normed_grad = lax.dot_general(key_back, key_w, contract, preferred_element_type=jnp.float32)
    normed_grad = normed_grad + lax.dot_general(value_cot, value_w, contract, preferred_element_type=jnp.float32)
    both = jnp.concatenate([key_back, value_cot], axis=1)
    term = lax.dot_general(normed, both, (((0,), (0,)), ((), ())), preferred_element_type=jnp.float32)
    gain_term = lax.optimization_barrier(jnp.sum(normed_grad * floats * inv_scale, axis=0))
    upstream = normed_grad * gain[None, :]
    inner = lax.optimization_barrier(jnp.mean(upstream * floats, axis=1, keepdims=True))
    grad_rows = (inv_scale * upstream - floats * inv_scale ** 3 * inner).astype(jnp.bfloat16)
    return (keys_out, values_out, grad_rows, term, gain_term)

def reference(tokens, norm_gain, key_weight, value_weight, key_cotangent, value_cotangent):
    count = TOKENS // SEQ
    cosine, sine = tables(SEQ)
    width = tokens.shape[1]
    feats = key_weight.shape[1]

    def step(carry, pieces):
        rows, key_cot, value_cot = pieces
        keys_out, values_out, grad_rows, term, gain_term = sequence_pass(rows, key_cot, value_cot, norm_gain, key_weight, value_weight, cosine, sine)
        return ((carry[0] + term, carry[1] + gain_term), (keys_out, values_out, grad_rows))
    start = (jnp.zeros((width, 2 * feats), jnp.float32), jnp.zeros((width,), jnp.float32))
    pieces = (tokens.reshape(count, SEQ, width), key_cotangent.reshape(count, SEQ, feats), value_cotangent.reshape(count, SEQ, feats))
    totals, stacked = lax.scan(step, start, pieces)
    term_sum = totals[0] / count
    gain_grad = totals[1] / count
    rotated_keys = stacked[0].reshape(TOKENS, feats)
    value_rows = stacked[1].reshape(TOKENS, feats)
    input_grad = stacked[2].reshape(TOKENS, width)
    return (rotated_keys, value_rows, input_grad, term_sum[:, :feats], term_sum[:, feats:], gain_grad)
```

```python
import math

import jax
import jax.numpy as jnp
import numpy as np
from jax import lax
from jax.experimental import pallas as pl
from jax.experimental.pallas import tpu as pltpu
from jax.sharding import Mesh, PartitionSpec as P

HEAD = 128
AXES = ("x", "zh", "c", "y", "zl")
SIZES = (4, 2, 2, 4, 2)
F32 = jnp.float32
BF16 = jnp.bfloat16
MIB = 1 << 20


def send(value, move):
    pairs = []
    for i in range(math.prod(SIZES)):
        x, zh, c, y, zl = (int(v) for v in np.unravel_index(i, SIZES))
        x, y, z, c = move(x, y, zh * 2 + zl, c)
        x, y, z, c = x % 4, y % 4, z % 4, c % 2
        pairs.append((i, int(np.ravel_multi_index((x, z // 2, c, y, z % 2), SIZES))))
    return lax.ppermute(value, AXES, pairs)


def to_core(value):
    return send(value, lambda x, y, z, c: (x, y, z, c + 1))


def to_x(value, d):
    return send(value, lambda x, y, z, c: (x + d, y, z, c))


def to_y(value, d):
    return send(value, lambda x, y, z, c: (x, y + d, z, c))


def to_z(value, d):
    return send(value, lambda x, y, z, c: (x, y, z + d, c))


def to_zl(value):
    return send(value, lambda x, y, z, c: (x, y, z ^ 1, c))


def params(mib, **more):
    return pltpu.CompilerParams(vmem_limit_bytes=mib * MIB, **more)


def turn(values, cosine, sine, direction):
    parts = []
    for h in range(values.shape[1] // HEAD):
        v = values[:, h * HEAD : (h + 1) * HEAD]
        parts.append(v * cosine + direction * (pltpu.roll(v, HEAD // 2, 1) * sine))
    return jnp.concatenate(parts, axis=1)


def norm_kernel(tok_ref, gain_ref, kc_ref, cos_ref, sin_ref, normed_ref, back_ref, inv_ref):
    v = tok_ref[...].astype(F32)
    inv = lax.rsqrt(jnp.mean(v * v, axis=1, keepdims=True) + 1e-05)
    normed_ref[...] = (v * inv * gain_ref[...]).astype(BF16)
    inv_ref[...] = jnp.broadcast_to(inv, inv_ref.shape)
    back_ref[...] = turn(kc_ref[...].astype(F32), cos_ref[...], sin_ref[...], -1.0).astype(BF16)


def norm(tokens, gain, key_cot, cosine, sine):
    rows, width = tokens.shape
    feats = key_cot.shape[1]
    tb = 128
    return pl.pallas_call(
        norm_kernel,
        grid=(rows // tb,),
        in_specs=[
            pl.BlockSpec((tb, width), lambda i: (i, 0)),
            pl.BlockSpec((1, width), lambda i: (0, 0)),
            pl.BlockSpec((tb, feats), lambda i: (i, 0)),
            pl.BlockSpec((tb, HEAD), lambda i: (i, 0)),
            pl.BlockSpec((tb, HEAD), lambda i: (i, 0)),
        ],
        out_specs=[
            pl.BlockSpec((tb, width), lambda i: (i, 0)),
            pl.BlockSpec((tb, feats), lambda i: (i, 0)),
            pl.BlockSpec((tb, HEAD), lambda i: (i, 0)),
        ],
        out_shape=[
            jax.ShapeDtypeStruct((rows, width), BF16),
            jax.ShapeDtypeStruct((rows, feats), BF16),
            jax.ShapeDtypeStruct((rows, HEAD), F32),
        ],
        compiler_params=params(24),
        cost_estimate=pl.CostEstimate(flops=8 * rows * width, bytes_accessed=4 * rows * width, transcendentals=0),
        name="norm",
    )(tokens, gain, key_cot, cosine, sine)


def terms(normed_ref, cot_ref):
    return lax.dot_general(normed_ref[...], cot_ref[...], (((0,), (0,)), ((), ())), preferred_element_type=F32)


def term_cost(rows, feats):
    return pl.CostEstimate(flops=2 * rows * 2048 * feats, bytes_accessed=6 * MIB, transcendentals=0)


def sibling_kernel(order_ref, normed_ref, cot_ref, out_ref):
    out_ref[0] = terms(normed_ref, cot_ref).astype(BF16)


def sibling_terms(order, normed, cot):
    rows, feats = cot.shape
    return pl.pallas_call(
        sibling_kernel,
        grid_spec=pltpu.PrefetchScalarGridSpec(
            num_scalar_prefetch=1,
            grid=(8,),
            in_specs=[
                pl.BlockSpec((rows, 256), lambda g, order: (0, order[g])),
                pl.BlockSpec((rows, feats), lambda g, order: (0, 0)),
            ],
            out_specs=pl.BlockSpec((1, 256, feats), lambda g, order: (g, 0, 0)),
        ),
        out_shape=jax.ShapeDtypeStruct((8, 256, feats), BF16),
        compiler_params=params(16),
        cost_estimate=term_cost(rows, feats),
        name="sibling_terms",
    )(order, normed, cot)


def own_kernel(parts, order_ref, normed_ref, cot_ref, got_ref, *out_refs):
    g = pl.program_id(0)
    each = 8 // parts
    total = (terms(normed_ref, cot_ref) + got_ref[0].astype(F32)).astype(BF16)
    for p in range(parts):

        @pl.when(g // each == p)
        def _():
            out_refs[p][0] = total


def own_terms(order, normed, cot, got, parts):
    rows, feats = cot.shape
    each = 8 // parts
    return pl.pallas_call(
        lambda *refs: own_kernel(parts, *refs),
        grid_spec=pltpu.PrefetchScalarGridSpec(
            num_scalar_prefetch=1,
            grid=(8,),
            in_specs=[
                pl.BlockSpec((rows, 256), lambda g, order: (0, order[g])),
                pl.BlockSpec((rows, feats), lambda g, order: (0, 0)),
                pl.BlockSpec((1, 256, feats), lambda g, order: (g, 0, 0)),
            ],
            out_specs=[
                pl.BlockSpec((1, 256, feats), lambda g, order, p=p: (jnp.clip(g - p * each, 0, each - 1), 0, 0))
                for p in range(parts)
            ],
        ),
        out_shape=[jax.ShapeDtypeStruct((each, 256, feats), BF16) for _ in range(parts)],
        compiler_params=params(24),
        cost_estimate=term_cost(rows, feats),
        name="own_terms",
    )(order, normed, cot, got)


def forward_kernel(normed_ref, w_ref, back_ref, vc_ref, inv_ref, cos_ref, sin_ref, key_ref, value_ref, coef_ref):
    feats = back_ref.shape[1]
    pre = jnp.dot(normed_ref[...], w_ref[...], preferred_element_type=F32)
    key_pre, value_pre = pre[:, :feats], pre[:, feats:]
    key_ref[...] = turn(key_pre, cos_ref[...], sin_ref[...], 1.0).astype(BF16)
    value_ref[...] = value_pre.astype(BF16)
    inner = jnp.sum(
        key_pre * back_ref[...].astype(F32) + value_pre * vc_ref[...].astype(F32), axis=1, keepdims=True
    )
    inv = inv_ref[...]
    coef_ref[...] = inv * inv * (inner * (1.0 / normed_ref.shape[1]))


def forward(normed, weights, key_back, value_cot, inv, cosine, sine):
    rows, width = normed.shape
    feats = key_back.shape[1]
    tb = 256
    by_rows = lambda n: pl.BlockSpec((tb, n), lambda i: (i, 0))
    return pl.pallas_call(
        forward_kernel,
        grid=(rows // tb,),
        in_specs=[
            by_rows(width),
            pl.BlockSpec((width, 2 * feats), lambda i: (0, 0)),
            by_rows(feats),
            by_rows(feats),
            by_rows(HEAD),
            by_rows(HEAD),
            by_rows(HEAD),
        ],
        out_specs=[by_rows(feats), by_rows(feats), by_rows(HEAD)],
        out_shape=[
            jax.ShapeDtypeStruct((rows, feats), BF16),
            jax.ShapeDtypeStruct((rows, feats), BF16),
            jax.ShapeDtypeStruct((rows, HEAD), F32),
        ],
        compiler_params=params(36),
        cost_estimate=pl.CostEstimate(flops=4 * rows * width * feats, bytes_accessed=20 * MIB, transcendentals=0),
        name="forward",
    )(normed, weights, key_back, value_cot, inv, cosine, sine)


def backward_kernel(tok_ref, w_ref, back_ref, vc_ref, inv_ref, coef_ref, gain_ref, into_ref, out_ref):
    both = jnp.concatenate([back_ref[...], vc_ref[...]], axis=1)
    grad = lax.dot_general(both, w_ref[...], (((1,), (1,)), ((), ())), preferred_element_type=F32)
    upstream = grad * gain_ref[...]
    out_ref[...] = (inv_ref[:, :1] * upstream - tok_ref[...].astype(F32) * coef_ref[:, :1]).astype(BF16)


def backward(first, blocks, tokens, weights, key_back, value_cot, inv, coef, gain, into):
    rows, width = tokens.shape
    feats = key_back.shape[1]
    cb = 512
    whole = lambda n: pl.BlockSpec((rows, n), lambda i: (0, 0))
    columns = pl.BlockSpec((rows, cb), lambda i: (0, i + first))
    operands = [tokens, weights, key_back, value_cot, inv, coef, gain]
    specs = [
        columns,
        pl.BlockSpec((cb, 2 * feats), lambda i: (i + first, 0)),
        whole(feats),
        whole(feats),
        whole(HEAD),
        whole(HEAD),
        pl.BlockSpec((1, cb), lambda i: (0, i + first)),
    ]
    body, aliases = backward_kernel, {}
    if into is None:
        body = lambda *refs: backward_kernel(*refs[:7], None, refs[7])
    else:
        operands.append(into)
        specs.append(pl.BlockSpec(memory_space=pl.ANY))
        aliases = {7: 0}
    return pl.pallas_call(
        body,
        grid=(blocks,),
        in_specs=specs,
        out_specs=columns,
        out_shape=jax.ShapeDtypeStruct((rows, width), BF16),
        input_output_aliases=aliases,
        compiler_params=params(36),
        cost_estimate=pl.CostEstimate(
            flops=4 * rows * blocks * cb * feats, bytes_accessed=6 * rows * blocks * cb, transcendentals=0
        ),
        name="backward",
    )(*operands)


def paired(own, got):
    return (own + got[1]) + (got[0] + got[2])


def shards(tokens, norm_gain, key_weight, value_weight, key_cotangent, value_cotangent):
    length, width = tokens.shape
    feats = key_weight.shape[1]
    count = math.prod(SIZES)
    x, zh, core, y = (lax.axis_index(a) for a in ("x", "zh", "c", "y"))
    half = HEAD // 2
    angles = np.arange(length)[:, None] * np.exp(-(2.0 * np.arange(half) / HEAD) * math.log(500000.0))[None, :]
    cosine = jnp.asarray(np.concatenate([np.cos(angles), np.cos(angles)], 1).astype(np.float32))
    sine = jnp.asarray(np.concatenate([-np.sin(angles), np.sin(angles)], 1).astype(np.float32))
    gain = norm_gain.reshape(1, width)

    shard = jnp.concatenate([key_weight, value_weight], axis=1)
    weights = lax.all_gather(shard, ("x", "zh", "c"), axis=0, tiled=True)

    normed, key_back, inv = norm(tokens, gain, key_cotangent, cosine, sine)

    i4, j2 = jnp.arange(4, dtype=jnp.int32), jnp.arange(2, dtype=jnp.int32)
    base = ((x + i4) % 4)[:, None] * 4 + ((zh + j2) % 2)[None, :] * 2
    x_major, z_major = base.reshape(8), base.T.reshape(8)
    sib_value = to_core(sibling_terms(x_major + 1 - core, normed, value_cotangent))
    sib_key = to_core(sibling_terms(z_major + 1 - core, normed, key_back))
    value_terms = own_terms(x_major + core, normed, value_cotangent, sib_value, 4)
    key_terms = own_terms(z_major + core, normed, key_back, sib_key, 2)

    got_x = [to_x(value_terms[d], d) for d in (1, 2, 3)]
    got_z = to_z(key_terms[1], 2)
    value_sum = value_terms[0].astype(F32) + sum(g.astype(F32) for g in got_x)
    key_sum = key_terms[0].astype(F32) + got_z.astype(F32)
    got_z = to_z(value_sum[1].astype(BF16), 2)
    got_x = [to_x(key_sum[d].astype(BF16), d) for d in (1, 2, 3)]
    value_part = value_sum[0] + got_z.astype(F32)
    key_part = key_sum[0] + sum(g.astype(F32) for g in got_x)

    parts = jnp.stack([key_part, value_part]).reshape(2, 4, 64, feats)
    piece = lambda d: lax.dynamic_index_in_dim(parts, (y + d) % 4, 1, keepdims=False)
    got_y = [to_y(piece(d).astype(BF16), d) for d in (1, 2, 3)]
    mine = (piece(0) + sum(g.astype(F32) for g in got_y)).astype(BF16)
    mine = ((mine.astype(F32) + to_zl(mine).astype(F32)) / count).astype(BF16)
    pieces = [mine] + [to_y(mine, d) for d in (1, 2, 3)]
    grads = jnp.zeros((2, 4, 64, feats), F32)
    for d, piece_d in enumerate(pieces):
        grads = lax.dynamic_update_slice(grads, piece_d.astype(F32)[:, None], (0, (y - d) % 4, 0, 0))
    key_grad, value_grad = grads[0].reshape(256, feats), grads[1].reshape(256, feats)

    first_row = (x * 4 + zh * 2 + core) * 256
    own_gain = lax.dynamic_slice(norm_gain, (first_row,), (256,))
    local = jnp.sum(key_part * key_weight.astype(F32) + value_part * value_weight.astype(F32), axis=1)
    total = lax.dynamic_update_slice(jnp.zeros((width,), F32), local / own_gain / count, (first_row,)).reshape(32, 128)
    total = total + to_core(total)
    total = paired(total, [to_x(total, d) for d in (1, 2, 3)])
    total = paired(total, [to_y(total, d) for d in (1, 2, 3)])
    total = paired(total, [to_z(total, d) for d in (1, 2, 3)])
    gain_grad = total.reshape(width)

    rotated_keys, value_rows, coef = forward(normed, weights, key_back, value_cotangent, inv, cosine, sine)
    input_grad = None
    for q in range(4):
        input_grad = backward(
            2 * q, 2, tokens, weights, key_back, value_cotangent, inv, coef, gain, input_grad
        )
    return rotated_keys, value_rows, input_grad, key_grad, value_grad, gain_grad


def solution(mesh):
    fine = Mesh(mesh.devices.reshape(SIZES), AXES)
    fsdp, replica = ("x", "zh", "c"), ("y", "zl")
    in_specs = (P(fsdp + replica, None), P(), P(fsdp, None), P(fsdp, None), P(fsdp + replica, None), P(fsdp + replica, None))
    out_specs = (P(fsdp + replica, None), P(fsdp + replica, None), P(fsdp + replica, None), P(fsdp, None), P(fsdp, None), P())
    return jax.shard_map(shards, mesh=fine, in_specs=in_specs, out_specs=out_specs, check_vma=False)
```

```python
import math

import jax
import jax.numpy as jnp
import numpy as np
from jax import lax
from jax.experimental import pallas as pl
from jax.experimental.pallas import tpu as pltpu
from jax.sharding import Mesh, PartitionSpec as P

HEAD = 128
AXES = ("x", "zh", "c", "y", "zl")
SIZES = (4, 2, 2, 4, 2)
F32 = jnp.float32
BF16 = jnp.bfloat16
MIB = 1 << 20


def send(value, move):
    pairs = []
    for i in range(math.prod(SIZES)):
        x, zh, c, y, zl = (int(v) for v in np.unravel_index(i, SIZES))
        x, y, z, c = move(x, y, zh * 2 + zl, c)
        x, y, z, c = x % 4, y % 4, z % 4, c % 2
        pairs.append((i, int(np.ravel_multi_index((x, z // 2, c, y, z % 2), SIZES))))
    return lax.ppermute(value, AXES, pairs)


def to_core(value):
    return send(value, lambda x, y, z, c: (x, y, z, c + 1))


def to_x(value, d):
    return send(value, lambda x, y, z, c: (x + d, y, z, c))


def to_y(value, d):
    return send(value, lambda x, y, z, c: (x, y + d, z, c))


def to_z(value, d):
    return send(value, lambda x, y, z, c: (x, y, z + d, c))


def to_zl(value):
    return send(value, lambda x, y, z, c: (x, y, z ^ 1, c))


def params(mib, **more):
    return pltpu.CompilerParams(vmem_limit_bytes=mib * MIB, **more)


def turn(values, cosine, sine, direction):
    parts = []
    for h in range(values.shape[1] // HEAD):
        v = values[:, h * HEAD : (h + 1) * HEAD]
        parts.append(v * cosine + direction * (pltpu.roll(v, HEAD // 2, 1) * sine))
    return jnp.concatenate(parts, axis=1)


RESIDENT = pl.BlockSpec(memory_space=pltpu.VMEM)
UNREAD = pl.BlockSpec(memory_space=pl.ANY)


def in_hbm(value):
    return pltpu.with_memory_space_constraint(value, pltpu.HBM)


def norm_kernel(
    order_ref, tok_ref, gain_ref, kc_ref, vc_ref, cos_ref, sin_ref, after_ref,
    both_out_ref, inv_ref, stored_ref, sib_v_ref, sib_k_ref, own_v_ref, own_k_ref, normed_ref, both_ref, done,
):
    i = pl.program_id(0)
    tb, feats = kc_ref.shape
    store = pltpu.make_async_copy(normed_ref, stored_ref, done)

    @pl.when(i < 4)
    def _():
        def rows(r, carry):
            at = pl.ds(pl.multiple_of(r * 16, 16), 16)
            v = tok_ref[at, :].astype(F32)
            inv = lax.rsqrt(jnp.mean(v * v, axis=1, keepdims=True) + 1e-05)
            inv_ref[at, :] = jnp.broadcast_to(inv, (16, HEAD))
            to = pl.ds(pl.multiple_of(i * tb + r * 16, 16), 16)
            normed_ref[to, :] = (tok_ref[at, :].astype(F32) * inv * gain_ref[...]).astype(BF16)
            return carry

        lax.fori_loop(0, tb // 16, rows, 0, unroll=2)
        here = pl.ds(pl.multiple_of(i * tb, tb), tb)
        back = turn(kc_ref[...].astype(F32), cos_ref[...], sin_ref[...], -1.0).astype(BF16)
        both_ref[here, :feats] = back
        both_ref[here, feats:] = vc_ref[...]
        both_out_ref[:, :feats] = back
        both_out_ref[:, feats:] = vc_ref[...]

    @pl.when(i == 4)
    def _():
        store.start()

    def part(value_ref, key_ref):
        for j in range(2):
            columns = pl.ds(pl.multiple_of(order_ref[(i - 4) * 2 + j] * 256, 256), 256)
            total = lax.dot_general(
                normed_ref[:, columns], both_ref[...], (((0,), (0,)), ((), ())), preferred_element_type=F32
            )
            key_ref[j] = total[:, :feats].astype(BF16)
            value_ref[j] = total[:, feats:].astype(BF16)

    pl.when((i >= 4) & (i < 8))(lambda: part(sib_v_ref, sib_k_ref))
    pl.when(i >= 8)(lambda: part(own_v_ref, own_k_ref))

    @pl.when(i == 11)
    def _():
        store.wait()


def norm_and_terms(order, tokens, gain, key_cot, value_cot, cosine, sine, after):
    rows, width = tokens.shape
    feats = key_cot.shape[1]
    tb = rows // 4
    by_rows = lambda n: pl.BlockSpec((tb, n), lambda i, order: (jnp.minimum(i, 3), 0))
    pairs = lambda first: pl.BlockSpec((2, 256, feats), lambda i, order: (jnp.clip(i - first, 0, 3), 0, 0))
    return pl.pallas_call(
        norm_kernel,
        grid_spec=pltpu.PrefetchScalarGridSpec(
            num_scalar_prefetch=1,
            grid=(12,),
            in_specs=[
                by_rows(width),
                pl.BlockSpec((1, width), lambda i, order: (0, 0)),
                by_rows(feats),
                by_rows(feats),
                by_rows(HEAD),
                by_rows(HEAD),
                UNREAD,
            ],
            out_specs=[by_rows(2 * feats), by_rows(HEAD), pl.BlockSpec(memory_space=pltpu.HBM)]
            + [pairs(4), pairs(4), pairs(8), pairs(8)],
            scratch_shapes=[
                pltpu.VMEM((rows, width), BF16),
                pltpu.VMEM((rows, 2 * feats), BF16),
                pltpu.SemaphoreType.DMA,
            ],
        ),
        out_shape=[
            pltpu.HBM((rows, 2 * feats), BF16),
            pltpu.HBM((rows, HEAD), F32),
            pltpu.HBM((rows, width), BF16),
        ]
        + [pltpu.HBM((8, 256, feats), BF16)] * 4,
        compiler_params=params(56),
        cost_estimate=pl.CostEstimate(flops=16000 * MIB, bytes_accessed=20 * MIB, transcendentals=0),
        name="norm_and_terms",
    )(order, in_hbm(tokens), gain, in_hbm(key_cot), in_hbm(value_cot), cosine, sine, in_hbm(after))


def add_values_kernel(y_ref, own_ref, got_ref, after_ref, *refs):
    out_refs, total_ref = refs[:4], refs[4]
    for j in range(own_ref.shape[0]):
        total_ref[...] = own_ref[j].astype(F32) + got_ref[j].astype(F32)
        for d in range(4):
            first = pl.multiple_of(lax.rem(y_ref[0] + d, 4) * 64, 64)
            out_refs[d][j] = total_ref[pl.ds(first, 64), :].astype(BF16)


def add_values(y, own, got, after):
    feats = own.shape[2]
    block = pl.BlockSpec((2, 256, feats), lambda g, y: (g, 0, 0))
    return pl.pallas_call(
        add_values_kernel,
        grid_spec=pltpu.PrefetchScalarGridSpec(
            num_scalar_prefetch=1,
            grid=(4,),
            in_specs=[block, block, UNREAD],
            out_specs=[pl.BlockSpec((2, 64, feats), lambda g, y: (g, 0, 0))] * 4,
            scratch_shapes=[pltpu.VMEM((256, feats), F32)],
        ),
        out_shape=[pltpu.HBM((8, 64, feats), BF16)] * 4,
        compiler_params=params(56),
        cost_estimate=pl.CostEstimate(flops=MIB, bytes_accessed=6 * MIB, transcendentals=0),
        name="add_values",
    )(y.reshape(1), in_hbm(own), in_hbm(got), in_hbm(after))


def add_keys_kernel(own_ref, got_ref, after_ref, near_ref, far_ref):
    for j, out_ref in enumerate((near_ref, far_ref)):
        out_ref[0] = (own_ref[j].astype(F32) + got_ref[j].astype(F32)).astype(BF16)


def add_keys(own, got, after):
    feats = own.shape[2]
    block = pl.BlockSpec((2, 256, feats), lambda g: (g, 0, 0))
    return pl.pallas_call(
        add_keys_kernel,
        grid=(4,),
        in_specs=[block, block, UNREAD],
        out_specs=[pl.BlockSpec((1, 256, feats), lambda g: (g, 0, 0))] * 2,
        out_shape=[pltpu.HBM((4, 256, feats), BF16)] * 2,
        compiler_params=params(56),
        cost_estimate=pl.CostEstimate(flops=MIB, bytes_accessed=6 * MIB, transcendentals=0),
        name="add_keys",
    )(in_hbm(own), in_hbm(got), in_hbm(after))


def forward_kernel(normed_ref, both_ref, inv_ref, cos_ref, sin_ref, w_ref, after_ref, key_ref, value_ref, coef_ref, held_ref, done):
    feats = key_ref.shape[1]
    parts = done.shape[0]
    depth = w_ref.shape[0] // parts
    first_step = pl.program_id(0) == 0
    at = [pl.ds(p * depth, depth) for p in range(parts)]
    copies = [pltpu.make_async_copy(w_ref.at[at[p], :], held_ref.at[at[p], :], done.at[p]) for p in range(parts)]

    @pl.when(first_step)
    def _():
        for copy in copies:
            copy.start()

    pre = None
    for p in range(parts):
        pl.when(first_step)(copies[p].wait)
        term = jnp.dot(normed_ref[:, at[p]], held_ref[at[p], :], preferred_element_type=F32)
        pre = term if pre is None else pre + term
    key_pre, value_pre = pre[:, :feats], pre[:, feats:]
    key_ref[...] = turn(key_pre, cos_ref[...], sin_ref[...], 1.0).astype(BF16)
    value_ref[...] = value_pre.astype(BF16)
    inner = jnp.sum(
        key_pre * both_ref[:, :feats].astype(F32) + value_pre * both_ref[:, feats:].astype(F32), axis=1, keepdims=True
    )
    inv = inv_ref[...]
    coef_ref[...] = inv * inv * (inner * (1.0 / normed_ref.shape[1]))


def forward(normed, both, inv, cosine, sine, weights, after):
    rows, width = normed.shape
    feats = both.shape[1] // 2
    tb = 256
    by_rows = lambda n: pl.BlockSpec((tb, n), lambda i: (i, 0))
    return pl.pallas_call(
        forward_kernel,
        grid=(rows // tb,),
        in_specs=[by_rows(width), by_rows(2 * feats), by_rows(HEAD), by_rows(HEAD), by_rows(HEAD), UNREAD, UNREAD],
        out_specs=[by_rows(feats), by_rows(feats), by_rows(HEAD)],
        scratch_shapes=[pltpu.VMEM(weights.shape, BF16), pltpu.SemaphoreType.DMA((4,))],
        out_shape=[
            pltpu.HBM((rows, feats), BF16),
            pltpu.HBM((rows, feats), BF16),
            pltpu.HBM((rows, HEAD), F32),
        ],
        compiler_params=params(56),
        cost_estimate=pl.CostEstimate(flops=4 * rows * width * feats, bytes_accessed=20 * MIB, transcendentals=0),
        name="forward",
    )(in_hbm(normed), in_hbm(both), in_hbm(inv), cosine, sine, in_hbm(weights), in_hbm(after))


def backward_kernel(tok_ref, both_ref, inv_ref, coef_ref, gain_ref, w_ref, after_ref, *refs):
    out_ref = refs[-1]
    for h in range(w_ref.shape[0] // 256):
        s = slice(h * 256, h * 256 + 256)
        grad = lax.dot_general(both_ref[...], w_ref[s], (((1,), (1,)), ((), ())), preferred_element_type=F32)
        out = inv_ref[:, :1] * (grad * gain_ref[:, s]) - tok_ref[:, s].astype(F32) * coef_ref[:, :1]
        out_ref[:, s] = out.astype(BF16)


def backward(first, blocks, tokens, both, inv, coef, gain, weights, into, after):
    rows, width = tokens.shape
    feats = both.shape[1] // 2
    cb = 512
    whole = lambda n: pl.BlockSpec((rows, n), lambda i: (0, 0))
    columns = pl.BlockSpec((rows, cb), lambda i: (0, i + first))
    operands = [in_hbm(tokens), in_hbm(both), in_hbm(inv), in_hbm(coef), gain, in_hbm(weights), in_hbm(after)]
    specs = [
        columns,
        whole(2 * feats),
        whole(HEAD),
        whole(HEAD),
        pl.BlockSpec((1, cb), lambda i: (0, i + first)),
        pl.BlockSpec((cb, 2 * feats), lambda i: (i + first, 0)),
        UNREAD,
    ]
    aliases = {}
    if into is not None:
        aliases = {len(operands): 0}
        operands.append(in_hbm(into))
        specs.append(UNREAD)
    return pl.pallas_call(
        backward_kernel,
        grid=(blocks,),
        in_specs=specs,
        out_specs=columns,
        out_shape=pltpu.HBM((rows, width), BF16),
        input_output_aliases=aliases,
        compiler_params=params(56),
        cost_estimate=pl.CostEstimate(
            flops=4 * blocks * rows * cb * feats, bytes_accessed=6 * blocks * rows * cb, transcendentals=0
        ),
        name="backward",
    )(*operands)


def total_of(refs):
    total = refs[0][...].astype(F32)
    for ref in refs[1:]:
        total += ref[...].astype(F32)
    return total


def join(kernel, name, operands, shapes, after=(), scalars=(), place=in_hbm):
    specs = [pl.BlockSpec(memory_space=pltpu.SMEM)] * len(scalars) + [RESIDENT] * len(operands) + [UNREAD] * len(after)
    return pl.pallas_call(
        kernel,
        in_specs=specs,
        out_specs=[RESIDENT] * len(shapes),
        out_shape=shapes,
        compiler_params=params(56),
        cost_estimate=pl.CostEstimate(flops=2 * MIB, bytes_accessed=4 * MIB, transcendentals=0),
        name=name,
    )(*scalars, *(place(o) for o in operands), *(in_hbm(a) for a in after))


def join_first_kernel(v0, v1, v2, v3, k0, k1, own_ref, *out_refs):
    for d in range(4):
        values = v0[2 * d : 2 * d + 2].astype(F32)
        for v in (v1, v2, v3):
            values += v[2 * d : 2 * d + 2].astype(F32)
        keys = k0[d].astype(F32) + k1[d].astype(F32)
        out_ref = own_ref if d == 0 else out_refs[d - 1]
        out_ref[:2] = values.astype(out_ref.dtype)
        for q in range(4):
            out_ref[2 + q] = keys[q * 64 : q * 64 + 64].astype(out_ref.dtype)


def join_x_kernel(y_ref, own, x1, x2, x3, value_ref, key_ref, to_z_ref, *to_y_refs):
    def sum_of(i):
        return own[i] + (x1[i].astype(F32) + x2[i].astype(F32) + x3[i].astype(F32))

    value_ref[...] = sum_of(0)
    to_z_ref[...] = sum_of(1).astype(BF16)
    for d in range(4):
        part = sum_of(2 + lax.rem(y_ref[0] + d, 4))
        if d == 0:
            key_ref[...] = part
        else:
            to_y_refs[d - 1][...] = part.astype(BF16)


def join_zy_kernel(value, z1, key, y1, y2, y3, after_ref, out_ref):
    out_ref[0] = total_of([key, y1, y2, y3]).astype(BF16)
    out_ref[1] = total_of([value, z1]).astype(BF16)


def join_zl_kernel(count, mine, other, out_ref):
    out_ref[...] = (total_of([mine, other]) * (1.0 / count)).astype(BF16)


def finish_kernel(y_ref, p0_ref, p1_ref, p2_ref, p3_ref, kw_ref, vw_ref, gain_ref, after_ref, key_ref, value_ref, g_ref):
    for d, p_ref in enumerate((p0_ref, p1_ref, p2_ref, p3_ref)):
        first = pl.multiple_of(lax.rem(y_ref[0] + 4 - d, 4) * 64, 64)
        key_ref[pl.ds(first, 64), :] = p_ref[0].astype(F32)
        value_ref[pl.ds(first, 64), :] = p_ref[1].astype(F32)
    products = key_ref[...] * kw_ref[...].astype(F32) + value_ref[...] * vw_ref[...].astype(F32)
    sums = jnp.broadcast_to(jnp.sum(products, axis=1, keepdims=True), (products.shape[0], HEAD))
    g_ref[...] = jnp.broadcast_to(sums.T[:1] / gain_ref[...], g_ref.shape)


def finish(y, pieces, key_weight, value_weight, own_gain, after):
    rows, feats = key_weight.shape
    return pl.pallas_call(
        finish_kernel,
        in_specs=[pl.BlockSpec(memory_space=pltpu.SMEM)] + [RESIDENT] * 7 + [UNREAD],
        out_specs=[RESIDENT] * 3,
        out_shape=[
            jax.ShapeDtypeStruct((rows, feats), F32),
            jax.ShapeDtypeStruct((rows, feats), F32),
            jax.ShapeDtypeStruct((16, rows), F32),
        ],
        compiler_params=params(56),
        cost_estimate=pl.CostEstimate(flops=4 * rows * feats, bytes_accessed=8 * rows * feats, transcendentals=0),
        name="finish",
    )(y.reshape(1), *pieces, key_weight, value_weight, own_gain, in_hbm(after))


def shards(tokens, norm_gain, key_weight, value_weight, key_cotangent, value_cotangent):
    length, width = tokens.shape
    feats = key_weight.shape[1]
    count = math.prod(SIZES)
    x, zh, core, y = (lax.axis_index(a).astype(jnp.int32) for a in ("x", "zh", "c", "y"))
    half = HEAD // 2
    angles = np.arange(length)[:, None] * np.exp(-(2.0 * np.arange(half) / HEAD) * math.log(500000.0))[None, :]
    cosine = jnp.asarray(np.concatenate([np.cos(angles), np.cos(angles)], 1).astype(np.float32))
    sine = jnp.asarray(np.concatenate([-np.sin(angles), np.sin(angles)], 1).astype(np.float32))
    gain = norm_gain.reshape(1, width)

    shard = jnp.concatenate([key_weight, value_weight], axis=1)
    weights = lax.all_gather(shard, ("x", "zh", "c"), axis=0, tiled=True)

    shape = pltpu.HBM
    i4, j2 = jnp.arange(4, dtype=jnp.int32), jnp.arange(2, dtype=jnp.int32)
    order = (((x + i4) % 4)[:, None] * 4 + ((zh + j2) % 2)[None, :] * 2).reshape(8)
    order = jnp.concatenate([order + 1 - core, order + core])
    both, inv, normed, sib_v, sib_k, own_v, own_k = norm_and_terms(
        order, tokens, gain, key_cotangent, value_cotangent, cosine, sine, shard
    )
    got_v, got_k = to_core(sib_v), to_core(sib_k)
    value_terms = add_values(y, own_v, got_v, inv)
    key_near, key_far = add_keys(own_k, got_k, value_terms[0])
    ring = lambda value: send(value, lambda x, y, z, c: (x + 1 - 2 * c, y, z, c))
    piece = shape((64, feats), BF16)
    got_y = [to_y(value_terms[d], d) for d in (1, 2, 3)]
    got_z = to_z(key_far, 2)
    own, *for_x = join(
        join_first_kernel,
        "join_first",
        [value_terms[0], *got_y, key_near, got_z],
        [shape((6, 64, feats), F32)] + [shape((6, 64, feats), BF16)] * 3,
    )
    got_x = [to_x(for_x[d - 1], d) for d in (1, 2, 3)]
    value_part, key_part, for_z, *for_y = join(
        join_x_kernel,
        "join_x",
        [own, *got_x],
        [shape((64, feats), F32)] * 2 + [piece] * 4,
        [],
        [y.reshape(1)],
    )
    got_z = to_z(for_z, 2)
    got_y = [to_y(for_y[d - 1], d) for d in (1, 2, 3)]
    rotated_keys, value_rows, coef = forward(normed, both, inv, cosine, sine, weights, for_z)
    pair = [shape((2, 64, feats), BF16)]
    (mine,) = join(join_zy_kernel, "join_zy", [value_part, got_z, key_part, *got_y], pair, [coef])
    (mine,) = join(lambda *refs: join_zl_kernel(count, *refs), "join_zl", [mine, to_zl(mine)], pair)
    parts = [mine] + [to_y(mine, d) for d in (1, 2, 3)]
    input_grad = backward(0, 4, tokens, both, inv, coef, gain, weights, None, mine)

    own_gain = lax.dynamic_slice(gain, (0, (x * 4 + zh * 2 + core) * 256), (1, 256))
    key_grad, value_grad, gain_rows = finish(y, parts, key_weight, value_weight, own_gain, input_grad)
    gain_grad = lax.all_to_all(gain_rows, ("x", "zh", "c"), 0, 0, tiled=True).reshape(width)
    input_grad = backward(4, 4, tokens, both, inv, coef, gain, weights, input_grad, gain_rows)
    return rotated_keys, value_rows, input_grad, key_grad, value_grad, gain_grad


def solution(mesh):
    fine = Mesh(mesh.devices.reshape(SIZES), AXES)
    fsdp, replica = ("x", "zh", "c"), ("y", "zl")
    in_specs = (P(fsdp + replica, None), P(), P(fsdp, None), P(fsdp, None), P(fsdp + replica, None), P(fsdp + replica, None))
    out_specs = (P(fsdp + replica, None), P(fsdp + replica, None), P(fsdp + replica, None), P(fsdp, None), P(fsdp, None), P())
    return jax.shard_map(shards, mesh=fine, in_specs=in_specs, out_specs=out_specs, check_vma=False)
```

```python
import math

import jax
import jax.numpy as jnp
import numpy as np
from jax import lax
from jax.experimental import pallas as pl
from jax.experimental.pallas import tpu as pltpu
from jax.sharding import Mesh, PartitionSpec as P

HEAD = 128
AXES = ("x", "zh", "c", "y", "zl")
SIZES = (4, 2, 2, 4, 2)
F32 = jnp.float32
BF16 = jnp.bfloat16
MIB = 1 << 20


def send(value, move):
    pairs = []
    for i in range(math.prod(SIZES)):
        x, zh, c, y, zl = (int(v) for v in np.unravel_index(i, SIZES))
        x, y, z, c = move(x, y, zh * 2 + zl, c)
        x, y, z, c = x % 4, y % 4, z % 4, c % 2
        pairs.append((i, int(np.ravel_multi_index((x, z // 2, c, y, z % 2), SIZES))))
    return lax.ppermute(value, AXES, pairs)


def to_core(value):
    return send(value, lambda x, y, z, c: (x, y, z, c + 1))


def params(mib, **more):
    return pltpu.CompilerParams(vmem_limit_bytes=mib * MIB, **more)


def turn(values, cosine, sine, direction):
    parts = []
    for h in range(values.shape[1] // HEAD):
        v = values[:, h * HEAD : (h + 1) * HEAD]
        parts.append(v * cosine + direction * (pltpu.roll(v, HEAD // 2, 1) * sine))
    return jnp.concatenate(parts, axis=1)


RESIDENT = pl.BlockSpec(memory_space=pltpu.VMEM)
UNREAD = pl.BlockSpec(memory_space=pl.ANY)


def in_hbm(value):
    return pltpu.with_memory_space_constraint(value, pltpu.HBM)


COLUMNS = (((0,), (0,)), ((), ()))


def norm_kernel(
    order_ref, tok_ref, gain_ref, kc_ref, vc_ref, cos_ref, sin_ref, after_ref,
    both_out_ref, inv_ref, stored_ref, t0_ref, t1_ref, t2_ref, t3_ref, normed_ref, both_ref, done,
):
    i = pl.program_id(0)
    tb, feats = kc_ref.shape
    store = pltpu.make_async_copy(normed_ref, stored_ref, done)

    @pl.when(i < 4)
    def _():
        def rows(r, carry):
            at = pl.ds(pl.multiple_of(r * 16, 16), 16)
            v = tok_ref[at, :].astype(F32)
            inv = lax.rsqrt(jnp.mean(v * v, axis=1, keepdims=True) + 1e-05)
            inv_ref[at, :] = jnp.broadcast_to(inv, (16, HEAD))
            to = pl.ds(pl.multiple_of(i * tb + r * 16, 16), 16)
            normed_ref[to, :] = (tok_ref[at, :].astype(F32) * inv * gain_ref[...]).astype(BF16)
            return carry

        lax.fori_loop(0, tb // 16, rows, 0, unroll=2)
        here = pl.ds(pl.multiple_of(i * tb, tb), tb)
        back = turn(kc_ref[...].astype(F32), cos_ref[...], sin_ref[...], -1.0).astype(BF16)
        both_ref[here, :feats] = back
        both_ref[here, feats:] = vc_ref[...]
        both_out_ref[:, :feats] = back
        both_out_ref[:, feats:] = vc_ref[...]

    @pl.when(i == 4)
    def _():
        store.start()

    def part(p, terms_ref):
        for j in range(2):
            columns = pl.ds(pl.multiple_of(order_ref[p * 2 + j] * 256, 256), 256)
            term = lax.dot_general(normed_ref[:, columns], both_ref[...], COLUMNS, preferred_element_type=F32)
            terms_ref[j] = term.astype(BF16)

    for p, terms_ref in enumerate((t0_ref, t1_ref, t2_ref, t3_ref)):
        pl.when(i == 4 + p)(lambda p=p, terms_ref=terms_ref: part(p, terms_ref))

    @pl.when(i == 7)
    def _():
        store.wait()


def norm_and_terms(order, tokens, gain, key_cot, value_cot, cosine, sine, after):
    rows, width = tokens.shape
    feats = key_cot.shape[1]
    tb = rows // 4
    by_rows = lambda n: pl.BlockSpec((tb, n), lambda i, order: (jnp.minimum(i, 3), 0))
    return pl.pallas_call(
        norm_kernel,
        grid_spec=pltpu.PrefetchScalarGridSpec(
            num_scalar_prefetch=1,
            grid=(8,),
            in_specs=[
                by_rows(width),
                pl.BlockSpec((1, width), lambda i, order: (0, 0)),
                by_rows(feats),
                by_rows(feats),
                by_rows(HEAD),
                by_rows(HEAD),
                UNREAD,
            ],
            out_specs=[
                by_rows(2 * feats),
                by_rows(HEAD),
                pl.BlockSpec(memory_space=pltpu.HBM),
            ]
            + [pl.BlockSpec((2, 256, 2 * feats), lambda i, order: (0, 0, 0))] * 4,
            scratch_shapes=[
                pltpu.VMEM((rows, width), BF16),
                pltpu.VMEM((rows, 2 * feats), BF16),
                pltpu.SemaphoreType.DMA,
            ],
        ),
        out_shape=[
            pltpu.HBM((rows, 2 * feats), BF16),
            pltpu.HBM((rows, HEAD), F32),
            pltpu.HBM((rows, width), BF16),
        ]
        + [pltpu.HBM((2, 256, 2 * feats), BF16)] * 4,
        compiler_params=params(56),
        cost_estimate=pl.CostEstimate(flops=10000 * MIB, bytes_accessed=20 * MIB, transcendentals=0),
        name="norm_and_terms",
    )(order, in_hbm(tokens), gain, in_hbm(key_cot), in_hbm(value_cot), cosine, sine, in_hbm(after))


def own_kernel(order_ref, n0_ref, n1_ref, both_ref, terms_ref):
    for j, n_ref in enumerate((n0_ref, n1_ref)):
        term = lax.dot_general(n_ref[...], both_ref[...], COLUMNS, preferred_element_type=F32)
        terms_ref[j] = term.astype(BF16)


def own_terms(order, normed, both):
    rows, feats = both.shape
    block = lambda j: pl.BlockSpec((rows, 256), lambda g, order: (0, order[2 * g + j]))
    return pl.pallas_call(
        own_kernel,
        grid_spec=pltpu.PrefetchScalarGridSpec(
            num_scalar_prefetch=1,
            grid=(4,),
            in_specs=[block(0), block(1), pl.BlockSpec((rows, feats), lambda g, order: (0, 0))],
            out_specs=pl.BlockSpec((2, 256, feats), lambda g, order: (g, 0, 0)),
        ),
        out_shape=pltpu.HBM((8, 256, feats), BF16),
        compiler_params=params(56),
        cost_estimate=pl.CostEstimate(flops=0, bytes_accessed=0, transcendentals=0),
        name="own_terms",
    )(order, in_hbm(normed), in_hbm(normed), in_hbm(both))


def add_kernel(own_ref, *refs):
    got_refs, out_ref = refs[:4], refs[-1]
    for p, got_ref in enumerate(got_refs):

        @pl.when(pl.program_id(0) == p)
        def _():
            out_ref[...] = (own_ref[...].astype(F32) + got_ref[...].astype(F32)).astype(BF16)


def add(own, got, after):
    block = pl.BlockSpec((2, *own.shape[1:]), lambda g: (g, 0, 0))
    fixed = pl.BlockSpec((2, *own.shape[1:]), lambda g: (0, 0, 0))
    return pl.pallas_call(
        add_kernel,
        grid=(4,),
        in_specs=[block] + [fixed] * 4 + [UNREAD],
        out_specs=block,
        out_shape=pltpu.HBM(own.shape, BF16),
        compiler_params=params(56),
        cost_estimate=pl.CostEstimate(flops=0, bytes_accessed=0, transcendentals=0),
        name="add",
    )(in_hbm(own), *(in_hbm(g) for g in got), in_hbm(after))


def pick_kernel(half_ref, value_ref, after_ref, same_ref, half_out_ref, done):
    rows = half_out_ref.shape[0]
    copy = pltpu.make_async_copy(value_ref.at[pl.ds(half_ref[0] * rows, rows)], half_out_ref, done)
    copy.start()
    copy.wait()


def pick(half, value, after):
    return pl.pallas_call(
        pick_kernel,
        in_specs=[pl.BlockSpec(memory_space=pltpu.SMEM), UNREAD, UNREAD],
        out_specs=[pl.BlockSpec(memory_space=pltpu.HBM)] * 2,
        out_shape=[pltpu.HBM(value.shape, BF16), pltpu.HBM((value.shape[0] // 2, *value.shape[1:]), BF16)],
        scratch_shapes=[pltpu.SemaphoreType.DMA],
        input_output_aliases={1: 0},
        cost_estimate=pl.CostEstimate(flops=0, bytes_accessed=2 * MIB, transcendentals=0),
        name="pick",
    )(half.reshape(1), in_hbm(value), in_hbm(after))


def forward_kernel(
    place_ref, normed_ref, both_ref, inv_ref, cos_ref, sin_ref, *refs
):
    w_refs, (key_ref, value_ref, coef_ref, held_ref, done) = refs[:6], refs[7:]
    feats = key_ref.shape[1]
    zh, core, zl = place_ref[0], place_ref[1], place_ref[2]
    first_step = pl.program_id(0) == 0
    copies = []
    for p, w_ref in enumerate(w_refs):
        c = lax.rem(core + p % 2, 2)
        if p < 2:
            to = held_ref.at[:, zh, c]
        else:
            to = held_ref.at[pl.ds(2 * lax.rem(zl + p // 2 - 1, 2), 2), 1 - zh, c]
        copies.append(pltpu.make_async_copy(w_ref, to, done.at[p]))

    @pl.when(first_step)
    def _():
        for copy in copies:
            copy.start()

    pre = None
    for z in range(2):
        for copy in copies[:2] if z == 0 else copies[2:]:
            pl.when(first_step)(copy.wait)
        at = lax.rem(zh + z, 2)
        for x in range(4):
            columns = pl.ds(pl.multiple_of(x * 1024 + at * 512, 512), 512)
            w = held_ref[x, at].reshape(512, 2 * feats)
            term = jnp.dot(normed_ref[:, columns], w, preferred_element_type=F32)
            pre = term if pre is None else pre + term
    key_pre, value_pre = pre[:, :feats], pre[:, feats:]
    key_ref[...] = turn(key_pre, cos_ref[...], sin_ref[...], 1.0).astype(BF16)
    value_ref[...] = value_pre.astype(BF16)
    inner = jnp.sum(
        key_pre * both_ref[:, :feats].astype(F32) + value_pre * both_ref[:, feats:].astype(F32), axis=1, keepdims=True
    )
    inv = inv_ref[...]
    coef_ref[...] = inv * inv * (inner * (1.0 / normed_ref.shape[1]))


def forward(place, normed, both, inv, cosine, sine, weights, after):
    rows, width = normed.shape
    feats = both.shape[1] // 2
    tb = 256
    by_rows = lambda n: pl.BlockSpec((tb, n), lambda i, place: (i, 0))
    return pl.pallas_call(
        forward_kernel,
        grid_spec=pltpu.PrefetchScalarGridSpec(
            num_scalar_prefetch=1,
            grid=(rows // tb,),
            in_specs=[by_rows(width), by_rows(2 * feats), by_rows(HEAD), by_rows(HEAD), by_rows(HEAD)] + [UNREAD] * 7,
            out_specs=[by_rows(feats), by_rows(feats), by_rows(HEAD)],
            scratch_shapes=[pltpu.VMEM((4, 2, 2, 256, 2 * feats), BF16), pltpu.SemaphoreType.DMA((6,))],
        ),
        out_shape=[
            pltpu.HBM((rows, feats), BF16),
            pltpu.HBM((rows, feats), BF16),
            pltpu.HBM((rows, HEAD), F32),
        ],
        compiler_params=params(56),
        cost_estimate=pl.CostEstimate(flops=4 * rows * width * feats, bytes_accessed=20 * MIB, transcendentals=0),
        name="forward",
    )(place, in_hbm(normed), in_hbm(both), in_hbm(inv), cosine, sine, *(in_hbm(w) for w in weights), in_hbm(after))


def backward_kernel(place_ref, tok_ref, both_ref, inv_ref, coef_ref, gain_ref, *refs):
    w_refs, out_ref = refs[:6], refs[6]

    def part(pair):
        for c, w_ref in enumerate(pair):
            s = pl.ds(pl.multiple_of(lax.rem(place_ref[8] + c, 2) * 256, 256), 256)
            grad = lax.dot_general(both_ref[...], w_ref[0], (((1,), (1,)), ((), ())), preferred_element_type=F32)
            out = inv_ref[:, :1] * (grad * gain_ref[:, s]) - tok_ref[:, s].astype(F32) * coef_ref[:, :1]
            out_ref[:, s] = out.astype(BF16)

    i = pl.program_id(0)
    pl.when(i < 4)(lambda: part(w_refs[:2]))
    pl.when((i >= 4) & (i < 6))(lambda: part(w_refs[2:4]))
    pl.when(i >= 6)(lambda: part(w_refs[4:]))


def backward(place, tokens, both, inv, coef, gain, weights):
    rows, width = tokens.shape
    feats = both.shape[1] // 2
    cb = 512
    whole = lambda n: pl.BlockSpec((rows, n), lambda i, place: (0, 0))
    columns = pl.BlockSpec((rows, cb), lambda i, place: (0, place[i]))
    block = lambda first, size: pl.BlockSpec(
        (1, 256, 2 * feats), lambda i, place: (jnp.clip(i - first, 0, size - 1), 0, 0)
    )
    return pl.pallas_call(
        backward_kernel,
        grid_spec=pltpu.PrefetchScalarGridSpec(
            num_scalar_prefetch=1,
            grid=(width // cb,),
            in_specs=[
                columns,
                whole(2 * feats),
                whole(HEAD),
                whole(HEAD),
                pl.BlockSpec((1, cb), lambda i, place: (0, place[i])),
                block(0, 4),
                block(0, 4),
                block(4, 2),
                block(4, 2),
                block(6, 2),
                block(6, 2),
            ],
            out_specs=columns,
        ),
        out_shape=pltpu.HBM((rows, width), BF16),
        compiler_params=params(56),
        cost_estimate=pl.CostEstimate(flops=4 * rows * width * feats, bytes_accessed=28 * MIB, transcendentals=0),
        name="backward",
    )(place, in_hbm(tokens), in_hbm(both), in_hbm(inv), in_hbm(coef), gain, *(in_hbm(w) for w in weights))


def total_kernel(count, got_ref, kw_ref, vw_ref, gain_ref, after_ref, out_ref, gain_out_ref, sum_ref):
    g = pl.program_id(0)
    feats = kw_ref.shape[1]
    part = got_ref[0].astype(F32)
    for j in range(1, got_ref.shape[0]):
        part += got_ref[j].astype(F32)

    @pl.when(g == 0)
    def _():
        sum_ref[...] = part

    @pl.when(g > 0)
    def _():
        sum_ref[...] += part

    @pl.when(g == pl.num_programs(0) - 1)
    def _():
        mean = sum_ref[...] * (1.0 / count)
        out_ref[...] = jnp.broadcast_to(mean.astype(BF16)[None], out_ref.shape)
        products = mean[:, :feats] * kw_ref[...].astype(F32) + mean[:, feats:] * vw_ref[...].astype(F32)
        sums = jnp.broadcast_to(jnp.sum(products, axis=1, keepdims=True), (products.shape[0], HEAD)).T
        line = jnp.concatenate([sums[:1]] * (HEAD // sums.shape[1]), axis=1) / gain_ref[...]
        gain_out_ref[...] = jnp.broadcast_to(line, gain_out_ref.shape)


def total(count, got, key_rows, value_rows, gain_rows, after):
    sources, rows, width = got.shape
    feats = key_rows.shape[1]
    fixed = lambda shape: pl.BlockSpec(shape, lambda g: (0,) * len(shape))
    return pl.pallas_call(
        lambda *refs: total_kernel(count, *refs),
        grid=(4,),
        in_specs=[
            pl.BlockSpec((sources // 4, rows, width), lambda g: (g, 0, 0)),
            fixed((rows, feats)),
            fixed((rows, feats)),
            fixed((1, HEAD)),
            UNREAD,
        ],
        out_specs=[fixed((8, rows, width)), fixed((count, HEAD))],
        out_shape=[pltpu.HBM((8, rows, width), BF16), pltpu.HBM((count, HEAD), F32)],
        scratch_shapes=[pltpu.VMEM((rows, width), F32)],
        compiler_params=params(56),
        cost_estimate=pl.CostEstimate(flops=2 * MIB, bytes_accessed=5 * MIB, transcendentals=0),
        name="total",
    )(in_hbm(got), key_rows, value_rows, gain_rows, in_hbm(after))


def finish_kernel(got_ref, key_ref, value_ref):
    feats = key_ref.shape[1]
    rows = got_ref[...].reshape(key_ref.shape[0], 2 * feats).astype(F32)
    key_ref[...] = rows[:, :feats]
    value_ref[...] = rows[:, feats:]


def finish(got):
    pieces, rows, width = got.shape
    vmem = pl.BlockSpec(memory_space=pltpu.VMEM)
    return pl.pallas_call(
        finish_kernel,
        in_specs=[vmem],
        out_specs=[vmem] * 2,
        out_shape=[pltpu.HBM((pieces * rows, width // 2), F32)] * 2,
        compiler_params=params(56),
        cost_estimate=pl.CostEstimate(flops=MIB, bytes_accessed=2 * MIB, transcendentals=0),
        name="finish",
    )(got)


def shards(tokens, norm_gain, key_weight, value_weight, key_cotangent, value_cotangent):
    length, width = tokens.shape
    feats = key_weight.shape[1]
    count = math.prod(SIZES)
    x, zh, core, y, zl = (lax.axis_index(a).astype(jnp.int32) for a in AXES)
    half = HEAD // 2
    angles = np.arange(length)[:, None] * np.exp(-(2.0 * np.arange(half) / HEAD) * math.log(500000.0))[None, :]
    cosine = jnp.asarray(np.concatenate([np.cos(angles), np.cos(angles)], 1).astype(np.float32))
    sine = jnp.asarray(np.concatenate([-np.sin(angles), np.sin(angles)], 1).astype(np.float32))
    gain = norm_gain.reshape(1, width)

    shard = jnp.concatenate([key_weight, value_weight], axis=1)
    spread = jnp.broadcast_to(shard[None], (4, 256, 2 * feats))
    near = lax.all_to_all(spread, "x", 0, 0, tiled=True)

    blocks = jnp.arange(8, dtype=jnp.int32) * 2
    both, inv, normed, *sibling = norm_and_terms(
        blocks + 1 - core, tokens, gain, key_cotangent, value_cotangent, cosine, sine, spread
    )
    sibling = [to_core(s) for s in sibling]
    terms = add(own_terms(blocks + core, normed, both), sibling, near)
    got = lax.all_to_all(terms.reshape(64, 32, 2 * feats), ("x", "zh", "y", "zl"), 0, 0, tiled=True)

    near, half_near = pick(1 - zl, near, terms)
    first = send(half_near, lambda x, y, z, c: (x, y, 3 - z, c))
    second = send(first, lambda x, y, z, c: (x, y, z ^ 1, c))
    weights = [near, to_core(near), first, to_core(first), second, to_core(second)]
    rotated_keys, value_rows, coef = forward(
        jnp.stack([zh, core, zl]), normed, both, inv, cosine, sine, weights, terms
    )
    i4, i2 = jnp.arange(4, dtype=jnp.int32), jnp.arange(2, dtype=jnp.int32)
    place = jnp.concatenate(
        [i4 * 2 + zh, (2 * zl + i2) * 2 + 1 - zh, (2 - 2 * zl + i2) * 2 + 1 - zh, core.reshape(1)]
    )
    input_grad = backward(place, tokens, both, inv, coef, gain, weights)

    row = (y * 2 + zl) * 32
    key_rows, value_rows_of = (lax.dynamic_slice(w, (row, 0), (32, feats)) for w in (key_weight, value_weight))
    own_gain = lax.dynamic_slice(norm_gain, ((x * 4 + zh * 2 + core) * 256 + row,), (32,))
    mean, gain_rows = total(count, got, key_rows, value_rows_of, jnp.tile(own_gain, 4).reshape(1, HEAD), input_grad)
    got = lax.all_to_all(mean, ("y", "zl"), 0, 0, tiled=True)
    gain_rows = lax.all_to_all(gain_rows, AXES, 0, 0, tiled=True)
    key_grad, value_grad = finish(got)
    return rotated_keys, value_rows, input_grad, key_grad, value_grad, gain_rows[:, :32].reshape(width)


def solution(mesh):
    fine = Mesh(mesh.devices.reshape(SIZES), AXES)
    fsdp, replica = ("x", "zh", "c"), ("y", "zl")
    in_specs = (P(fsdp + replica, None), P(), P(fsdp, None), P(fsdp, None), P(fsdp + replica, None), P(fsdp + replica, None))
    out_specs = (P(fsdp + replica, None), P(fsdp + replica, None), P(fsdp + replica, None), P(fsdp, None), P(fsdp, None), P())
    return jax.shard_map(shards, mesh=fine, in_specs=in_specs, out_specs=out_specs, check_vma=False)
```

```python
import math

import jax
import jax.numpy as jnp
import numpy as np
from jax import lax
from jax.experimental import pallas as pl
from jax.experimental.pallas import tpu as pltpu
from jax.sharding import Mesh, PartitionSpec as P

HEAD = 128
AXES = ("x", "zh", "c", "y", "zl")
SIZES = (4, 2, 2, 4, 2)
F32 = jnp.float32
BF16 = jnp.bfloat16
MIB = 1 << 20


def send(value, move):
    pairs = []
    for i in range(math.prod(SIZES)):
        x, zh, c, y, zl = (int(v) for v in np.unravel_index(i, SIZES))
        x, y, z, c = move(x, y, zh * 2 + zl, c)
        x, y, z, c = x % 4, y % 4, z % 4, c % 2
        pairs.append((i, int(np.ravel_multi_index((x, z // 2, c, y, z % 2), SIZES))))
    return lax.ppermute(value, AXES, pairs)


def to_core(value):
    return send(value, lambda x, y, z, c: (x, y, z, c + 1))


def params(mib, **more):
    return pltpu.CompilerParams(vmem_limit_bytes=mib * MIB, **more)


def turn(values, cosine, sine, direction):
    parts = []
    for h in range(values.shape[1] // HEAD):
        v = values[:, h * HEAD : (h + 1) * HEAD]
        parts.append(v * cosine + direction * (pltpu.roll(v, HEAD // 2, 1) * sine))
    return jnp.concatenate(parts, axis=1)


RESIDENT = pl.BlockSpec(memory_space=pltpu.VMEM)
UNREAD = pl.BlockSpec(memory_space=pl.ANY)


def in_hbm(value):
    return pltpu.with_memory_space_constraint(value, pltpu.HBM)


COLUMNS = (((0,), (0,)), ((), ()))


def norm_kernel(
    order_ref, tok_ref, gain_ref, kc_ref, vc_ref, cos_ref, sin_ref, after_ref,
    both_out_ref, inv_ref, stored_ref, t0_ref, t1_ref, t2_ref, t3_ref, normed_ref, both_ref, done,
):
    i = pl.program_id(0)
    tb, feats = kc_ref.shape
    store = pltpu.make_async_copy(normed_ref, stored_ref, done)

    @pl.when(i < 4)
    def _():
        def rows(r, carry):
            at = pl.ds(pl.multiple_of(r * 16, 16), 16)
            v = tok_ref[at, :].astype(F32)
            inv = lax.rsqrt(jnp.mean(v * v, axis=1, keepdims=True) + 1e-05)
            inv_ref[at, :] = jnp.broadcast_to(inv, (16, HEAD))
            to = pl.ds(pl.multiple_of(i * tb + r * 16, 16), 16)
            normed_ref[to, :] = (tok_ref[at, :].astype(F32) * inv * gain_ref[...]).astype(BF16)
            return carry

        lax.fori_loop(0, tb // 16, rows, 0, unroll=2)
        here = pl.ds(pl.multiple_of(i * tb, tb), tb)
        back = turn(kc_ref[...].astype(F32), cos_ref[...], sin_ref[...], -1.0).astype(BF16)
        both_ref[here, :feats] = back
        both_ref[here, feats:] = vc_ref[...]
        both_out_ref[:, :feats] = back
        both_out_ref[:, feats:] = vc_ref[...]

    @pl.when(i == 4)
    def _():
        store.start()

    def part(p, terms_ref):
        for j in range(2):
            columns = pl.ds(pl.multiple_of(order_ref[p * 2 + j] * 256, 256), 256)
            term = lax.dot_general(normed_ref[:, columns], both_ref[...], COLUMNS, preferred_element_type=F32)
            terms_ref[j] = term.astype(BF16)

    for p, terms_ref in enumerate((t0_ref, t1_ref, t2_ref, t3_ref)):
        pl.when(i == 4 + p)(lambda p=p, terms_ref=terms_ref: part(p, terms_ref))

    @pl.when(i == 7)
    def _():
        store.wait()


def norm_and_terms(order, tokens, gain, key_cot, value_cot, cosine, sine, after):
    rows, width = tokens.shape
    feats = key_cot.shape[1]
    tb = rows // 4
    by_rows = lambda n: pl.BlockSpec((tb, n), lambda i, order: (jnp.minimum(i, 3), 0))
    return pl.pallas_call(
        norm_kernel,
        grid_spec=pltpu.PrefetchScalarGridSpec(
            num_scalar_prefetch=1,
            grid=(8,),
            in_specs=[
                by_rows(width),
                pl.BlockSpec((1, width), lambda i, order: (0, 0)),
                by_rows(feats),
                by_rows(feats),
                by_rows(HEAD),
                by_rows(HEAD),
                UNREAD,
            ],
            out_specs=[
                by_rows(2 * feats),
                by_rows(HEAD),
                pl.BlockSpec(memory_space=pltpu.HBM),
            ]
            + [pl.BlockSpec((2, 256, 2 * feats), lambda i, order: (0, 0, 0))] * 4,
            scratch_shapes=[
                pltpu.VMEM((rows, width), BF16),
                pltpu.VMEM((rows, 2 * feats), BF16),
                pltpu.SemaphoreType.DMA,
            ],
        ),
        out_shape=[
            pltpu.HBM((rows, 2 * feats), BF16),
            pltpu.HBM((rows, HEAD), F32),
            pltpu.HBM((rows, width), BF16),
        ]
        + [pltpu.HBM((2, 256, 2 * feats), BF16)] * 4,
        compiler_params=params(56),
        cost_estimate=pl.CostEstimate(flops=10000 * MIB, bytes_accessed=20 * MIB, transcendentals=0),
        name="norm_and_terms",
    )(order, in_hbm(tokens), gain, in_hbm(key_cot), in_hbm(value_cot), cosine, sine, in_hbm(after))


def own_kernel(order_ref, n0_ref, n1_ref, both_ref, terms_ref):
    for j, n_ref in enumerate((n0_ref, n1_ref)):
        term = lax.dot_general(n_ref[...], both_ref[...], COLUMNS, preferred_element_type=F32)
        terms_ref[j] = term.astype(BF16)


def own_terms(order, normed, both):
    rows, feats = both.shape
    block = lambda j: pl.BlockSpec((rows, 256), lambda g, order: (0, order[2 * g + j]))
    return pl.pallas_call(
        own_kernel,
        grid_spec=pltpu.PrefetchScalarGridSpec(
            num_scalar_prefetch=1,
            grid=(4,),
            in_specs=[block(0), block(1), pl.BlockSpec((rows, feats), lambda g, order: (0, 0))],
            out_specs=pl.BlockSpec((2, 256, feats), lambda g, order: (g, 0, 0)),
        ),
        out_shape=pltpu.HBM((8, 256, feats), BF16),
        compiler_params=params(56),
        cost_estimate=pl.CostEstimate(flops=0, bytes_accessed=0, transcendentals=0),
        name="own_terms",
    )(order, in_hbm(normed), in_hbm(normed), in_hbm(both))


def add_kernel(own_ref, *refs):
    got_refs, out_ref = refs[:4], refs[-1]
    for p, got_ref in enumerate(got_refs):

        @pl.when(pl.program_id(0) == p)
        def _():
            out_ref[...] = (own_ref[...].astype(F32) + got_ref[...].astype(F32)).astype(BF16)


def add(own, got, after):
    block = pl.BlockSpec((2, *own.shape[1:]), lambda g: (g, 0, 0))
    fixed = pl.BlockSpec((2, *own.shape[1:]), lambda g: (0, 0, 0))
    return pl.pallas_call(
        add_kernel,
        grid=(4,),
        in_specs=[block] + [fixed] * 4 + [UNREAD],
        out_specs=block,
        out_shape=pltpu.HBM(own.shape, BF16),
        compiler_params=params(56),
        cost_estimate=pl.CostEstimate(flops=0, bytes_accessed=0, transcendentals=0),
        name="add",
    )(in_hbm(own), *(in_hbm(g) for g in got), in_hbm(after))


def release(value, after):
    return pl.pallas_call(
        lambda *refs: None,
        in_specs=[UNREAD] * 2,
        out_specs=pl.BlockSpec(memory_space=pltpu.HBM),
        out_shape=pltpu.HBM(value.shape, value.dtype),
        input_output_aliases={0: 0},
        cost_estimate=pl.CostEstimate(flops=0, bytes_accessed=0, transcendentals=0),
        name="release",
    )(in_hbm(value), in_hbm(after))


def forward_kernel(
    core_ref, normed_ref, both_ref, inv_ref, cos_ref, sin_ref, own_ref, other_ref, after_ref,
    key_ref, value_ref, coef_ref, held_ref, done,
):
    feats = key_ref.shape[1]
    first_step = pl.program_id(0) == 0
    copies = []
    for p in range(4):
        for c, w_ref in enumerate((own_ref, other_ref)):
            to = held_ref.at[pl.ds(2 * p, 2), lax.rem(core_ref[0] + c, 2)]
            copies.append(pltpu.make_async_copy(w_ref.at[pl.ds(2 * p, 2)], to, done.at[2 * p + c]))

    @pl.when(first_step)
    def _():
        for copy in copies:
            copy.start()

    pre = None
    for p in range(4):
        pl.when(first_step)(copies[2 * p].wait)
        pl.when(first_step)(copies[2 * p + 1].wait)
        w = held_ref[2 * p : 2 * p + 2].reshape(1024, 2 * feats)
        term = jnp.dot(normed_ref[:, p * 1024 : p * 1024 + 1024], w, preferred_element_type=F32)
        pre = term if pre is None else pre + term
    key_pre, value_pre = pre[:, :feats], pre[:, feats:]
    key_ref[...] = turn(key_pre, cos_ref[...], sin_ref[...], 1.0).astype(BF16)
    value_ref[...] = value_pre.astype(BF16)
    inner = jnp.sum(
        key_pre * both_ref[:, :feats].astype(F32) + value_pre * both_ref[:, feats:].astype(F32), axis=1, keepdims=True
    )
    inv = inv_ref[...]
    coef_ref[...] = inv * inv * (inner * (1.0 / normed_ref.shape[1]))


def forward(core, normed, both, inv, cosine, sine, own, other, after):
    rows, width = normed.shape
    feats = both.shape[1] // 2
    tb = 256
    by_rows = lambda n: pl.BlockSpec((tb, n), lambda i, core: (i, 0))
    return pl.pallas_call(
        forward_kernel,
        grid_spec=pltpu.PrefetchScalarGridSpec(
            num_scalar_prefetch=1,
            grid=(rows // tb,),
            in_specs=[by_rows(width), by_rows(2 * feats), by_rows(HEAD), by_rows(HEAD), by_rows(HEAD)] + [UNREAD] * 3,
            out_specs=[by_rows(feats), by_rows(feats), by_rows(HEAD)],
            scratch_shapes=[pltpu.VMEM((8, 2, 256, 2 * feats), BF16), pltpu.SemaphoreType.DMA((8,))],
        ),
        out_shape=[
            pltpu.HBM((rows, feats), BF16),
            pltpu.HBM((rows, feats), BF16),
            pltpu.HBM((rows, HEAD), F32),
        ],
        compiler_params=params(56),
        cost_estimate=pl.CostEstimate(flops=4 * rows * width * feats, bytes_accessed=20 * MIB, transcendentals=0),
        name="forward",
    )(core, in_hbm(normed), in_hbm(both), in_hbm(inv), cosine, sine, in_hbm(own), in_hbm(other), in_hbm(after))


def backward_kernel(core_ref, tok_ref, both_ref, inv_ref, coef_ref, gain_ref, own_ref, other_ref, out_ref):
    for c, w_ref in enumerate((own_ref, other_ref)):
        s = pl.ds(pl.multiple_of(lax.rem(core_ref[0] + c, 2) * 256, 256), 256)
        grad = lax.dot_general(both_ref[...], w_ref[0], (((1,), (1,)), ((), ())), preferred_element_type=F32)
        out = inv_ref[:, :1] * (grad * gain_ref[:, s]) - tok_ref[:, s].astype(F32) * coef_ref[:, :1]
        out_ref[:, s] = out.astype(BF16)


def backward(core, tokens, both, inv, coef, gain, own, other):
    rows, width = tokens.shape
    feats = both.shape[1] // 2
    cb = 512
    whole = lambda n: pl.BlockSpec((rows, n), lambda i, core: (0, 0))
    columns = pl.BlockSpec((rows, cb), lambda i, core: (0, i))
    weights = pl.BlockSpec((1, 256, 2 * feats), lambda i, core: (i, 0, 0))
    return pl.pallas_call(
        backward_kernel,
        grid_spec=pltpu.PrefetchScalarGridSpec(
            num_scalar_prefetch=1,
            grid=(width // cb,),
            in_specs=[
                columns,
                whole(2 * feats),
                whole(HEAD),
                whole(HEAD),
                pl.BlockSpec((1, cb), lambda i, core: (0, i)),
                weights,
                weights,
            ],
            out_specs=columns,
        ),
        out_shape=pltpu.HBM((rows, width), BF16),
        compiler_params=params(56),
        cost_estimate=pl.CostEstimate(flops=4 * rows * width * feats, bytes_accessed=28 * MIB, transcendentals=0),
        name="backward",
    )(core, in_hbm(tokens), in_hbm(both), in_hbm(inv), in_hbm(coef), gain, in_hbm(own), in_hbm(other))


def total_kernel(count, got_ref, kw_ref, vw_ref, gain_ref, after_ref, out_ref, gain_out_ref, sum_ref):
    g = pl.program_id(0)
    feats = kw_ref.shape[1]
    part = got_ref[0].astype(F32)
    for j in range(1, got_ref.shape[0]):
        part += got_ref[j].astype(F32)

    @pl.when(g == 0)
    def _():
        sum_ref[...] = part

    @pl.when(g > 0)
    def _():
        sum_ref[...] += part

    @pl.when(g == pl.num_programs(0) - 1)
    def _():
        mean = sum_ref[...] * (1.0 / count)
        out_ref[...] = mean.astype(BF16)
        products = mean[:, :feats] * kw_ref[...].astype(F32) + mean[:, feats:] * vw_ref[...].astype(F32)
        sums = jnp.broadcast_to(jnp.sum(products, axis=1, keepdims=True), (products.shape[0], HEAD)).T
        line = jnp.concatenate([sums[:1]] * (HEAD // sums.shape[1]), axis=1) / gain_ref[...]
        gain_out_ref[...] = jnp.broadcast_to(line, gain_out_ref.shape)


def total(count, got, key_rows, value_rows, gain_rows, after):
    sources, rows, width = got.shape
    feats = key_rows.shape[1]
    fixed = lambda shape: pl.BlockSpec(shape, lambda g: (0,) * len(shape))
    return pl.pallas_call(
        lambda *refs: total_kernel(count, *refs),
        grid=(4,),
        in_specs=[
            pl.BlockSpec((sources // 4, rows, width), lambda g: (g, 0, 0)),
            fixed((rows, feats)),
            fixed((rows, feats)),
            fixed((1, HEAD)),
            UNREAD,
        ],
        out_specs=[fixed((rows, width)), fixed((count, HEAD))],
        out_shape=[pltpu.HBM((rows, width), BF16), pltpu.HBM((count, HEAD), F32)],
        scratch_shapes=[pltpu.VMEM((rows, width), F32)],
        compiler_params=params(56),
        cost_estimate=pl.CostEstimate(flops=2 * MIB, bytes_accessed=5 * MIB, transcendentals=0),
        name="total",
    )(in_hbm(got), key_rows, value_rows, gain_rows, in_hbm(after))


def pair_kernel(zl_ref, mine_ref, got_ref, out_ref):
    out_ref[zl_ref[0]] = mine_ref[...]
    out_ref[1 - zl_ref[0]] = got_ref[...]


def pair(zl, mine, got):
    vmem = pl.BlockSpec(memory_space=pltpu.VMEM)
    return pl.pallas_call(
        pair_kernel,
        in_specs=[pl.BlockSpec(memory_space=pltpu.SMEM), vmem, vmem],
        out_specs=vmem,
        out_shape=jax.ShapeDtypeStruct((2, *mine.shape), BF16),
        compiler_params=params(8),
        cost_estimate=pl.CostEstimate(flops=0, bytes_accessed=0, transcendentals=0),
        name="pair",
    )(zl.reshape(1), mine, got)


def finish_kernel(y_ref, p0_ref, p1_ref, p2_ref, p3_ref, key_ref, value_ref):
    feats = key_ref.shape[1]
    for d, p_ref in enumerate((p0_ref, p1_ref, p2_ref, p3_ref)):
        for z in range(2):
            first = lax.rem(y_ref[0] + 4 - d, 4) * 64 + z * 32
            at = pl.ds(pl.multiple_of(first, 32), 32)
            key_ref[at, :] = p_ref[z, :, :feats].astype(F32)
            value_ref[at, :] = p_ref[z, :, feats:].astype(F32)


def finish(y, pieces):
    pairs, rows, width = pieces[0].shape
    vmem = pl.BlockSpec(memory_space=pltpu.VMEM)
    return pl.pallas_call(
        finish_kernel,
        in_specs=[pl.BlockSpec(memory_space=pltpu.SMEM)] + [vmem] * 4,
        out_specs=[vmem] * 2,
        out_shape=[pltpu.HBM((4 * pairs * rows, width // 2), F32)] * 2,
        compiler_params=params(8),
        cost_estimate=pl.CostEstimate(flops=MIB, bytes_accessed=2 * MIB, transcendentals=0),
        name="finish",
    )(y.reshape(1), *pieces)


def shards(tokens, norm_gain, key_weight, value_weight, key_cotangent, value_cotangent):
    length, width = tokens.shape
    feats = key_weight.shape[1]
    count = math.prod(SIZES)
    x, zh, core, y, zl = (lax.axis_index(a).astype(jnp.int32) for a in AXES)
    half = HEAD // 2
    angles = np.arange(length)[:, None] * np.exp(-(2.0 * np.arange(half) / HEAD) * math.log(500000.0))[None, :]
    cosine = jnp.asarray(np.concatenate([np.cos(angles), np.cos(angles)], 1).astype(np.float32))
    sine = jnp.asarray(np.concatenate([-np.sin(angles), np.sin(angles)], 1).astype(np.float32))
    gain = norm_gain.reshape(1, width)

    shard = jnp.concatenate([key_weight, value_weight], axis=1)
    spread = jnp.broadcast_to(shard[None], (8, 256, 2 * feats))
    own_weights = lax.all_to_all(spread, ("x", "zh"), 0, 0, tiled=True)

    blocks = jnp.arange(8, dtype=jnp.int32) * 2
    both, inv, normed, *sibling = norm_and_terms(
        blocks + 1 - core, tokens, gain, key_cotangent, value_cotangent, cosine, sine, spread
    )
    sibling = [to_core(s) for s in sibling]
    terms = add(own_terms(blocks + core, normed, both), sibling, inv)
    got = lax.all_to_all(terms.reshape(64, 32, 2 * feats), ("x", "zh", "y", "zl"), 0, 0, tiled=True)

    own_weights = release(own_weights, terms)
    other_weights = to_core(own_weights)
    at = core.reshape(1)
    rotated_keys, value_rows, coef = forward(
        at, normed, both, inv, cosine, sine, own_weights, other_weights, terms
    )
    input_grad = backward(at, tokens, both, inv, coef, gain, own_weights, other_weights)

    row = (y * 2 + zl) * 32
    key_rows, value_rows_of = (lax.dynamic_slice(w, (row, 0), (32, feats)) for w in (key_weight, value_weight))
    own_gain = lax.dynamic_slice(norm_gain, ((x * 4 + zh * 2 + core) * 256 + row,), (32,))
    mean, gain_rows = total(count, got, key_rows, value_rows_of, jnp.tile(own_gain, 4).reshape(1, HEAD), input_grad)
    gain_rows = lax.all_to_all(gain_rows, AXES, 0, 0, tiled=True)
    pieces = pair(zl, mean, send(mean, lambda x, y, z, c: (x, y, z ^ 1, c)))
    pieces = [pieces] + [send(pieces, lambda x, y, z, c, d=d: (x, y + d, z, c)) for d in (1, 2, 3)]
    key_grad, value_grad = finish(y, pieces)
    return rotated_keys, value_rows, input_grad, key_grad, value_grad, gain_rows[:, :32].reshape(width)


def solution(mesh):
    fine = Mesh(mesh.devices.reshape(SIZES), AXES)
    fsdp, replica = ("x", "zh", "c"), ("y", "zl")
    in_specs = (P(fsdp + replica, None), P(), P(fsdp, None), P(fsdp, None), P(fsdp + replica, None), P(fsdp + replica, None))
    out_specs = (P(fsdp + replica, None), P(fsdp + replica, None), P(fsdp + replica, None), P(fsdp, None), P(fsdp, None), P())
    return jax.shard_map(shards, mesh=fine, in_specs=in_specs, out_specs=out_specs, check_vma=False)
```

```python
import math

import jax
import jax.numpy as jnp
import numpy as np
from jax import lax
from jax.experimental import pallas as pl
from jax.experimental.pallas import tpu as pltpu
from jax.sharding import Mesh, PartitionSpec as P

HEAD = 128
AXES = ("x", "zh", "c", "y", "zl")
SIZES = (4, 2, 2, 4, 2)
F32 = jnp.float32
BF16 = jnp.bfloat16
MIB = 1 << 20


def send(value, move):
    pairs = []
    for i in range(math.prod(SIZES)):
        x, zh, c, y, zl = (int(v) for v in np.unravel_index(i, SIZES))
        x, y, z, c = move(x, y, zh * 2 + zl, c)
        x, y, z, c = x % 4, y % 4, z % 4, c % 2
        pairs.append((i, int(np.ravel_multi_index((x, z // 2, c, y, z % 2), SIZES))))
    return lax.ppermute(value, AXES, pairs)


def to_core(value):
    return send(value, lambda x, y, z, c: (x, y, z, c + 1))


def params(mib, **more):
    return pltpu.CompilerParams(vmem_limit_bytes=mib * MIB, **more)


def turn(values, cosine, sine, direction):
    parts = []
    for h in range(values.shape[1] // HEAD):
        v = values[:, h * HEAD : (h + 1) * HEAD]
        parts.append(v * cosine + direction * (pltpu.roll(v, HEAD // 2, 1) * sine))
    return jnp.concatenate(parts, axis=1)


RESIDENT = pl.BlockSpec(memory_space=pltpu.VMEM)
UNREAD = pl.BlockSpec(memory_space=pl.ANY)


def in_hbm(value):
    return pltpu.with_memory_space_constraint(value, pltpu.HBM)


COLUMNS = (((0,), (0,)), ((), ()))


def norm_kernel(
    order_ref, tok_ref, gain_ref, kc_ref, vc_ref, cos_ref, sin_ref, after_ref,
    both_out_ref, inv_ref, stored_ref, t0_ref, t1_ref, normed_ref, both_ref, done,
):
    i = pl.program_id(0)
    tb, feats = kc_ref.shape
    store = pltpu.make_async_copy(normed_ref, stored_ref, done)

    @pl.when(i < 4)
    def _():
        def rows(r, carry):
            at = pl.ds(pl.multiple_of(r * 16, 16), 16)
            v = tok_ref[at, :].astype(F32)
            inv = lax.rsqrt(jnp.mean(v * v, axis=1, keepdims=True) + 1e-05)
            inv_ref[at, :] = jnp.broadcast_to(inv, (16, HEAD))
            to = pl.ds(pl.multiple_of(i * tb + r * 16, 16), 16)
            normed_ref[to, :] = (tok_ref[at, :].astype(F32) * inv * gain_ref[...]).astype(BF16)
            return carry

        lax.fori_loop(0, tb // 16, rows, 0, unroll=2)
        here = pl.ds(pl.multiple_of(i * tb, tb), tb)
        back = turn(kc_ref[...].astype(F32), cos_ref[...], sin_ref[...], -1.0).astype(BF16)
        both_ref[here, :feats] = back
        both_ref[here, feats:] = vc_ref[...]
        both_out_ref[:, :feats] = back
        both_out_ref[:, feats:] = vc_ref[...]

    @pl.when(i == 4)
    def _():
        store.start()

    def part(p, terms_ref):
        for j in range(2):
            columns = pl.ds(pl.multiple_of(order_ref[p * 2 + j] * 256, 256), 256)
            term = lax.dot_general(normed_ref[:, columns], both_ref[...], COLUMNS, preferred_element_type=F32)
            terms_ref[p % 2 * 2 + j] = term.astype(BF16)

    for p in range(4):
        pl.when(i == 4 + p)(lambda p=p: part(p, (t0_ref, t1_ref)[p // 2]))

    @pl.when(i == 7)
    def _():
        store.wait()


def norm_and_terms(order, tokens, gain, key_cot, value_cot, cosine, sine, after):
    rows, width = tokens.shape
    feats = key_cot.shape[1]
    tb = rows // 4
    by_rows = lambda n: pl.BlockSpec((tb, n), lambda i, order: (jnp.minimum(i, 3), 0))
    return pl.pallas_call(
        norm_kernel,
        grid_spec=pltpu.PrefetchScalarGridSpec(
            num_scalar_prefetch=1,
            grid=(8,),
            in_specs=[
                by_rows(width),
                pl.BlockSpec((1, width), lambda i, order: (0, 0)),
                by_rows(feats),
                by_rows(feats),
                by_rows(HEAD),
                by_rows(HEAD),
                UNREAD,
            ],
            out_specs=[
                by_rows(2 * feats),
                by_rows(HEAD),
                pl.BlockSpec(memory_space=pltpu.HBM),
            ]
            + [pl.BlockSpec((4, 256, 2 * feats), lambda i, order: (0, 0, 0))] * 2,
            scratch_shapes=[
                pltpu.VMEM((rows, width), BF16),
                pltpu.VMEM((rows, 2 * feats), BF16),
                pltpu.SemaphoreType.DMA,
            ],
        ),
        out_shape=[
            pltpu.HBM((rows, 2 * feats), BF16),
            pltpu.HBM((rows, HEAD), F32),
            pltpu.HBM((rows, width), BF16),
        ]
        + [pltpu.HBM((4, 256, 2 * feats), BF16)] * 2,
        compiler_params=params(56),
        cost_estimate=pl.CostEstimate(flops=10000 * MIB, bytes_accessed=20 * MIB, transcendentals=0),
        name="norm_and_terms",
    )(order, in_hbm(tokens), gain, in_hbm(key_cot), in_hbm(value_cot), cosine, sine, in_hbm(after))


def own_kernel(order_ref, n0_ref, n1_ref, both_ref, after_ref, terms_ref):
    for j, n_ref in enumerate((n0_ref, n1_ref)):
        term = lax.dot_general(n_ref[...], both_ref[...], COLUMNS, preferred_element_type=F32)
        terms_ref[j] = term.astype(BF16)


def own_terms(order, normed, both, after):
    rows, feats = both.shape
    block = lambda j: pl.BlockSpec((rows, 256), lambda g, order: (0, order[2 * g + j]))
    return pl.pallas_call(
        own_kernel,
        grid_spec=pltpu.PrefetchScalarGridSpec(
            num_scalar_prefetch=1,
            grid=(4,),
            in_specs=[block(0), block(1), pl.BlockSpec((rows, feats), lambda g, order: (0, 0)), UNREAD],
            out_specs=pl.BlockSpec((2, 256, feats), lambda g, order: (g, 0, 0)),
        ),
        out_shape=pltpu.HBM((8, 256, feats), BF16),
        compiler_params=params(56),
        cost_estimate=pl.CostEstimate(flops=30000 * MIB, bytes_accessed=0, transcendentals=0),
        name="own_terms",
    )(order, in_hbm(normed), in_hbm(normed), in_hbm(both), in_hbm(after))


def add_kernel(own_ref, got0_ref, got1_ref, after_ref, out_ref):
    def part(got_ref):
        out_ref[...] = (own_ref[...].astype(F32) + got_ref[...].astype(F32)).astype(BF16)

    pl.when(pl.program_id(0) < 2)(lambda: part(got0_ref))
    pl.when(pl.program_id(0) >= 2)(lambda: part(got1_ref))


def add(own, got, after):
    block = lambda place: pl.BlockSpec((2, *own.shape[1:]), lambda g: (place(g), 0, 0))
    return pl.pallas_call(
        add_kernel,
        grid=(4,),
        in_specs=[
            block(lambda g: g),
            block(lambda g: jnp.minimum(g, 1)),
            block(lambda g: jnp.maximum(g - 2, 0)),
            UNREAD,
        ],
        out_specs=block(lambda g: g),
        out_shape=pltpu.HBM(own.shape, BF16),
        compiler_params=params(56),
        cost_estimate=pl.CostEstimate(flops=0, bytes_accessed=0, transcendentals=0),
        name="add",
    )(in_hbm(own), *(in_hbm(g) for g in got), in_hbm(after))


def release(values, after):
    n = len(values)
    return pl.pallas_call(
        lambda *refs: None,
        in_specs=[UNREAD] * (n + 1),
        out_specs=[pl.BlockSpec(memory_space=pltpu.HBM)] * n,
        out_shape=[pltpu.HBM(v.shape, v.dtype) for v in values],
        input_output_aliases={k: k for k in range(n)},
        cost_estimate=pl.CostEstimate(flops=0, bytes_accessed=0, transcendentals=0),
        name="release",
    )(*(in_hbm(v) for v in values), in_hbm(after))


def forward_kernel(
    place_ref, normed_ref, both_ref, inv_ref, cos_ref, sin_ref, *refs
):
    w_refs, (key_ref, value_ref, coef_ref, held_ref, done) = refs[:10], refs[11:]
    feats = key_ref.shape[1]
    zh, core, x_here = place_ref[0], place_ref[1], place_ref[2]
    first_step = pl.program_id(0) == 0
    copies = []
    for p, w_ref in enumerate(w_refs):
        c = lax.rem(core + p % 2, 2)
        if p < 2:
            to = held_ref.at[:, zh, c]
        else:
            to = held_ref.at[lax.rem(x_here + 5 - p // 2, 4), 1 - zh, c]
        copies.append(pltpu.make_async_copy(w_ref, to, done.at[p]))

    @pl.when(first_step)
    def _():
        for copy in copies:
            copy.start()

    pre = None
    for z in range(2):
        for copy in copies[:2] if z == 0 else copies[2:]:
            pl.when(first_step)(copy.wait)
        at = lax.rem(zh + z, 2)
        for x in range(4):
            columns = pl.ds(pl.multiple_of(x * 1024 + at * 512, 512), 512)
            w = held_ref[x, at].reshape(512, 2 * feats)
            term = jnp.dot(normed_ref[:, columns], w, preferred_element_type=F32)
            pre = term if pre is None else pre + term
    key_pre, value_pre = pre[:, :feats], pre[:, feats:]
    key_ref[...] = turn(key_pre, cos_ref[...], sin_ref[...], 1.0).astype(BF16)
    value_ref[...] = value_pre.astype(BF16)
    inner = jnp.sum(
        key_pre * both_ref[:, :feats].astype(F32) + value_pre * both_ref[:, feats:].astype(F32), axis=1, keepdims=True
    )
    inv = inv_ref[...]
    coef_ref[...] = inv * inv * (inner * (1.0 / normed_ref.shape[1]))


def forward(place, normed, both, inv, cosine, sine, weights, after):
    rows, width = normed.shape
    feats = both.shape[1] // 2
    tb = 256
    by_rows = lambda n: pl.BlockSpec((tb, n), lambda i, place: (i, 0))
    return pl.pallas_call(
        forward_kernel,
        grid_spec=pltpu.PrefetchScalarGridSpec(
            num_scalar_prefetch=1,
            grid=(rows // tb,),
            in_specs=[by_rows(width), by_rows(2 * feats), by_rows(HEAD), by_rows(HEAD), by_rows(HEAD)] + [UNREAD] * 11,
            out_specs=[by_rows(feats), by_rows(feats), by_rows(HEAD)],
            scratch_shapes=[pltpu.VMEM((4, 2, 2, 256, 2 * feats), BF16), pltpu.SemaphoreType.DMA((10,))],
        ),
        out_shape=[
            pltpu.HBM((rows, feats), BF16),
            pltpu.HBM((rows, feats), BF16),
            pltpu.HBM((rows, HEAD), F32),
        ],
        compiler_params=params(56),
        cost_estimate=pl.CostEstimate(flops=4 * rows * width * feats, bytes_accessed=20 * MIB, transcendentals=0),
        name="forward",
    )(place, in_hbm(normed), in_hbm(both), in_hbm(inv), cosine, sine, *(in_hbm(w) for w in weights), in_hbm(after))


def backward_kernel(place_ref, tok_ref, both_ref, inv_ref, coef_ref, gain_ref, *refs):
    w_refs, out_ref = refs[:10], refs[10]

    def part(pair):
        for c, w_ref in enumerate(pair):
            s = pl.ds(pl.multiple_of(lax.rem(place_ref[8] + c, 2) * 256, 256), 256)
            w = w_ref[...].reshape(256, both_ref.shape[1])
            grad = lax.dot_general(both_ref[...], w, (((1,), (1,)), ((), ())), preferred_element_type=F32)
            out = inv_ref[:, :1] * (grad * gain_ref[:, s]) - tok_ref[:, s].astype(F32) * coef_ref[:, :1]
            out_ref[:, s] = out.astype(BF16)

    i = pl.program_id(0)
    pl.when(i < 4)(lambda: part(w_refs[:2]))
    for d in range(4):
        pl.when(i == 4 + d)(lambda d=d: part(w_refs[2 + 2 * d : 4 + 2 * d]))


def backward(place, tokens, both, inv, coef, gain, weights):
    rows, width = tokens.shape
    feats = both.shape[1] // 2
    cb = 512
    whole = lambda n: pl.BlockSpec((rows, n), lambda i, place: (0, 0))
    columns = pl.BlockSpec((rows, cb), lambda i, place: (0, place[i]))
    block = pl.BlockSpec((1, 256, 2 * feats), lambda i, place: (jnp.minimum(i, 3), 0, 0))
    return pl.pallas_call(
        backward_kernel,
        grid_spec=pltpu.PrefetchScalarGridSpec(
            num_scalar_prefetch=1,
            grid=(width // cb,),
            in_specs=[
                columns,
                whole(2 * feats),
                whole(HEAD),
                whole(HEAD),
                pl.BlockSpec((1, cb), lambda i, place: (0, place[i])),
                block,
                block,
            ]
            + [pl.BlockSpec((256, 2 * feats), lambda i, place: (0, 0))] * 8,
            out_specs=columns,
        ),
        out_shape=pltpu.HBM((rows, width), BF16),
        compiler_params=params(56),
        cost_estimate=pl.CostEstimate(flops=4 * rows * width * feats, bytes_accessed=28 * MIB, transcendentals=0),
        name="backward",
    )(place, in_hbm(tokens), in_hbm(both), in_hbm(inv), in_hbm(coef), gain, *(in_hbm(w) for w in weights))


def total_kernel(count, got_ref, kw_ref, vw_ref, gain_ref, after_ref, out_ref, gain_out_ref, sum_ref):
    g = pl.program_id(0)
    feats = kw_ref.shape[1]
    part = got_ref[0].astype(F32)
    for j in range(1, got_ref.shape[0]):
        part += got_ref[j].astype(F32)

    @pl.when(g == 0)
    def _():
        sum_ref[...] = part

    @pl.when(g > 0)
    def _():
        sum_ref[...] += part

    @pl.when(g == pl.num_programs(0) - 1)
    def _():
        mean = sum_ref[...] * (1.0 / count)
        out_ref[...] = mean.astype(BF16)
        products = mean[:, :feats] * kw_ref[...].astype(F32) + mean[:, feats:] * vw_ref[...].astype(F32)
        sums = jnp.broadcast_to(jnp.sum(products, axis=1, keepdims=True), (products.shape[0], HEAD)).T
        line = jnp.concatenate([sums[:1]] * (HEAD // sums.shape[1]), axis=1) / gain_ref[...]
        gain_out_ref[...] = jnp.broadcast_to(line, gain_out_ref.shape)


def total(count, got, key_rows, value_rows, gain_rows, after):
    sources, rows, width = got.shape
    feats = key_rows.shape[1]
    fixed = lambda shape: pl.BlockSpec(shape, lambda g: (0,) * len(shape))
    return pl.pallas_call(
        lambda *refs: total_kernel(count, *refs),
        grid=(4,),
        in_specs=[
            pl.BlockSpec((sources // 4, rows, width), lambda g: (g, 0, 0)),
            fixed((rows, feats)),
            fixed((rows, feats)),
            fixed((1, HEAD)),
            UNREAD,
        ],
        out_specs=[fixed((rows, width)), fixed((count, HEAD))],
        out_shape=[pltpu.HBM((rows, width), BF16), pltpu.HBM((count, HEAD), F32)],
        scratch_shapes=[pltpu.VMEM((rows, width), F32)],
        compiler_params=params(56),
        cost_estimate=pl.CostEstimate(flops=2 * MIB, bytes_accessed=5 * MIB, transcendentals=0),
        name="total",
    )(in_hbm(got), key_rows, value_rows, gain_rows, in_hbm(after))


def pair_kernel(zl_ref, mine_ref, got_ref, out_ref):
    out_ref[zl_ref[0]] = mine_ref[...]
    out_ref[1 - zl_ref[0]] = got_ref[...]


def pair(zl, mine, got):
    vmem = pl.BlockSpec(memory_space=pltpu.VMEM)
    return pl.pallas_call(
        pair_kernel,
        in_specs=[pl.BlockSpec(memory_space=pltpu.SMEM), vmem, vmem],
        out_specs=vmem,
        out_shape=jax.ShapeDtypeStruct((2, *mine.shape), BF16),
        compiler_params=params(8),
        cost_estimate=pl.CostEstimate(flops=0, bytes_accessed=0, transcendentals=0),
        name="pair",
    )(zl.reshape(1), mine, got)


def finish_kernel(y_ref, p0_ref, p1_ref, p2_ref, p3_ref, key_ref, value_ref):
    feats = key_ref.shape[1]
    for d, p_ref in enumerate((p0_ref, p1_ref, p2_ref, p3_ref)):
        for z in range(2):
            first = lax.rem(y_ref[0] + 4 - d, 4) * 64 + z * 32
            at = pl.ds(pl.multiple_of(first, 32), 32)
            key_ref[at, :] = p_ref[z, :, :feats].astype(F32)
            value_ref[at, :] = p_ref[z, :, feats:].astype(F32)


def finish(y, pieces):
    pairs, rows, width = pieces[0].shape
    vmem = pl.BlockSpec(memory_space=pltpu.VMEM)
    return pl.pallas_call(
        finish_kernel,
        in_specs=[pl.BlockSpec(memory_space=pltpu.SMEM)] + [vmem] * 4,
        out_specs=[vmem] * 2,
        out_shape=[pltpu.HBM((4 * pairs * rows, width // 2), F32)] * 2,
        compiler_params=params(8),
        cost_estimate=pl.CostEstimate(flops=MIB, bytes_accessed=2 * MIB, transcendentals=0),
        name="finish",
    )(y.reshape(1), *pieces)


def shards(tokens, norm_gain, key_weight, value_weight, key_cotangent, value_cotangent):
    length, width = tokens.shape
    feats = key_weight.shape[1]
    count = math.prod(SIZES)
    x, zh, core, y, zl = (lax.axis_index(a).astype(jnp.int32) for a in AXES)
    half = HEAD // 2
    angles = np.arange(length)[:, None] * np.exp(-(2.0 * np.arange(half) / HEAD) * math.log(500000.0))[None, :]
    cosine = jnp.asarray(np.concatenate([np.cos(angles), np.cos(angles)], 1).astype(np.float32))
    sine = jnp.asarray(np.concatenate([-np.sin(angles), np.sin(angles)], 1).astype(np.float32))
    gain = norm_gain.reshape(1, width)

    shard = jnp.concatenate([key_weight, value_weight], axis=1)
    spread = jnp.broadcast_to(shard[None], (4, 256, 2 * feats))
    near = lax.all_to_all(spread, "x", 0, 0, tiled=True)
    far = send(shard, lambda x, y, z, c: (x, y, z + 2, c))
    far = [far] + [send(far, lambda x, y, z, c, d=d: (x + d, y, z, c)) for d in (1, 2, 3)]

    blocks = jnp.arange(8, dtype=jnp.int32) * 2
    both, inv, normed, *sibling = norm_and_terms(
        blocks + 1 - core, tokens, gain, key_cotangent, value_cotangent, cosine, sine, spread
    )
    sibling = [to_core(s) for s in sibling]
    terms = add(own_terms(blocks + core, normed, both, near), sibling, inv)
    terms, near, *far = release([terms, near, *far], inv)
    got = lax.all_to_all(terms.reshape(64, 32, 2 * feats), ("x", "zh", "y", "zl"), 0, 0, tiled=True)

    weights = [near, to_core(near)]
    for w in far:
        weights += [w, to_core(w)]
    rotated_keys, value_rows, coef = forward(
        jnp.stack([zh, core, x]), normed, both, inv, cosine, sine, weights, terms
    )
    i4 = jnp.arange(4, dtype=jnp.int32)
    place = jnp.concatenate([i4 * 2 + zh, (x + 4 - i4) % 4 * 2 + 1 - zh, core.reshape(1)])
    input_grad = backward(place, tokens, both, inv, coef, gain, weights)

    row = (y * 2 + zl) * 32
    key_rows, value_rows_of = (lax.dynamic_slice(w, (row, 0), (32, feats)) for w in (key_weight, value_weight))
    own_gain = lax.dynamic_slice(norm_gain, ((x * 4 + zh * 2 + core) * 256 + row,), (32,))
    mean, gain_rows = total(count, got, key_rows, value_rows_of, jnp.tile(own_gain, 4).reshape(1, HEAD), input_grad)
    gain_rows = lax.all_to_all(gain_rows, AXES, 0, 0, tiled=True)
    pieces = pair(zl, mean, send(mean, lambda x, y, z, c: (x, y, z ^ 1, c)))
    pieces = [pieces] + [send(pieces, lambda x, y, z, c, d=d: (x, y + d, z, c)) for d in (1, 2, 3)]
    key_grad, value_grad = finish(y, pieces)
    return rotated_keys, value_rows, input_grad, key_grad, value_grad, gain_rows[:, :32].reshape(width)


def solution(mesh):
    fine = Mesh(mesh.devices.reshape(SIZES), AXES)
    fsdp, replica = ("x", "zh", "c"), ("y", "zl")
    in_specs = (P(fsdp + replica, None), P(), P(fsdp, None), P(fsdp, None), P(fsdp + replica, None), P(fsdp + replica, None))
    out_specs = (P(fsdp + replica, None), P(fsdp + replica, None), P(fsdp + replica, None), P(fsdp, None), P(fsdp, None), P())
    return jax.shard_map(shards, mesh=fine, in_specs=in_specs, out_specs=out_specs, check_vma=False)
```

```python
import math

import jax
import jax.numpy as jnp
import numpy as np
from jax import lax
from jax.experimental import pallas as pl
from jax.experimental.pallas import tpu as pltpu
from jax.sharding import Mesh, PartitionSpec as P

HEAD = 128
AXES = ("x", "zh", "c", "y", "zl")
SIZES = (4, 2, 2, 4, 2)
F32 = jnp.float32
BF16 = jnp.bfloat16
MIB = 1 << 20


def send(value, move):
    pairs = []
    for i in range(math.prod(SIZES)):
        x, zh, c, y, zl = (int(v) for v in np.unravel_index(i, SIZES))
        x, y, z, c = move(x, y, zh * 2 + zl, c)
        x, y, z, c = x % 4, y % 4, z % 4, c % 2
        pairs.append((i, int(np.ravel_multi_index((x, z // 2, c, y, z % 2), SIZES))))
    return lax.ppermute(value, AXES, pairs)


def to_core(value):
    return send(value, lambda x, y, z, c: (x, y, z, c + 1))


def params(mib, **more):
    return pltpu.CompilerParams(vmem_limit_bytes=mib * MIB, **more)


def turn(values, cosine, sine, direction):
    parts = []
    for h in range(values.shape[1] // HEAD):
        v = values[:, h * HEAD : (h + 1) * HEAD]
        parts.append(v * cosine + direction * (pltpu.roll(v, HEAD // 2, 1) * sine))
    return jnp.concatenate(parts, axis=1)


RESIDENT = pl.BlockSpec(memory_space=pltpu.VMEM)
UNREAD = pl.BlockSpec(memory_space=pl.ANY)


def in_hbm(value):
    return pltpu.with_memory_space_constraint(value, pltpu.HBM)


COLUMNS = (((0,), (0,)), ((), ()))


def norm_kernel(
    order_ref, tok_ref, gain_ref, kc_ref, vc_ref, cos_ref, sin_ref, after_ref,
    both_out_ref, inv_ref, stored_ref, t0_ref, t1_ref, normed_ref, both_ref, done,
):
    i = pl.program_id(0)
    tb, feats = kc_ref.shape
    store = pltpu.make_async_copy(normed_ref, stored_ref, done)

    @pl.when(i < 4)
    def _():
        v = tok_ref[...].astype(F32)
        inv = lax.rsqrt(jnp.mean(v * v, axis=1, keepdims=True) + 1e-05)
        inv_ref[...] = jnp.broadcast_to(inv, inv_ref.shape)
        normed_ref[pl.ds(pl.multiple_of(i * tb, tb), tb), :] = (v * inv * gain_ref[...]).astype(BF16)
        here = pl.ds(pl.multiple_of(i * tb, tb), tb)
        back = turn(kc_ref[...].astype(F32), cos_ref[...], sin_ref[...], -1.0).astype(BF16)
        both_ref[here, :feats] = back
        both_ref[here, feats:] = vc_ref[...]
        both_out_ref[:, :feats] = back
        both_out_ref[:, feats:] = vc_ref[...]

    @pl.when(i == 4)
    def _():
        store.start()

    def part(p, terms_ref):
        for j in range(2):
            columns = pl.ds(pl.multiple_of(order_ref[p * 2 + j] * 256, 256), 256)
            term = lax.dot_general(normed_ref[:, columns], both_ref[...], COLUMNS, preferred_element_type=F32)
            terms_ref[p % 2 * 2 + j] = term.astype(BF16)

    for p in range(4):
        pl.when(i == 4 + p)(lambda p=p: part(p, (t0_ref, t1_ref)[p // 2]))

    @pl.when(i == 7)
    def _():
        store.wait()


def norm_and_terms(order, tokens, gain, key_cot, value_cot, cosine, sine, after):
    rows, width = tokens.shape
    feats = key_cot.shape[1]
    tb = rows // 4
    by_rows = lambda n: pl.BlockSpec((tb, n), lambda i, order: (jnp.minimum(i, 3), 0))
    return pl.pallas_call(
        norm_kernel,
        grid_spec=pltpu.PrefetchScalarGridSpec(
            num_scalar_prefetch=1,
            grid=(8,),
            in_specs=[
                by_rows(width),
                pl.BlockSpec((1, width), lambda i, order: (0, 0)),
                by_rows(feats),
                by_rows(feats),
                by_rows(HEAD),
                by_rows(HEAD),
                UNREAD,
            ],
            out_specs=[
                by_rows(2 * feats),
                by_rows(HEAD),
                pl.BlockSpec(memory_space=pltpu.HBM),
            ]
            + [pl.BlockSpec((4, 256, 2 * feats), lambda i, order: (0, 0, 0))] * 2,
            scratch_shapes=[
                pltpu.VMEM((rows, width), BF16),
                pltpu.VMEM((rows, 2 * feats), BF16),
                pltpu.SemaphoreType.DMA,
            ],
        ),
        out_shape=[
            pltpu.HBM((rows, 2 * feats), BF16),
            pltpu.HBM((rows, HEAD), F32),
            pltpu.HBM((rows, width), BF16),
        ]
        + [pltpu.HBM((4, 256, 2 * feats), BF16)] * 2,
        compiler_params=params(56),
        cost_estimate=pl.CostEstimate(flops=10000 * MIB, bytes_accessed=20 * MIB, transcendentals=0),
        name="norm_and_terms",
    )(order, in_hbm(tokens), gain, in_hbm(key_cot), in_hbm(value_cot), cosine, sine, in_hbm(after))


def own_kernel(order_ref, n0_ref, n1_ref, both_ref, after_ref, terms_ref):
    for j, n_ref in enumerate((n0_ref, n1_ref)):
        term = lax.dot_general(n_ref[...], both_ref[...], COLUMNS, preferred_element_type=F32)
        terms_ref[j] = term.astype(BF16)


def own_terms(order, normed, both, after):
    rows, feats = both.shape
    block = lambda j: pl.BlockSpec((rows, 256), lambda g, order: (0, order[2 * g + j]))
    return pl.pallas_call(
        own_kernel,
        grid_spec=pltpu.PrefetchScalarGridSpec(
            num_scalar_prefetch=1,
            grid=(4,),
            in_specs=[block(0), block(1), pl.BlockSpec((rows, feats), lambda g, order: (0, 0)), UNREAD],
            out_specs=pl.BlockSpec((2, 256, feats), lambda g, order: (g, 0, 0)),
        ),
        out_shape=pltpu.HBM((8, 256, feats), BF16),
        compiler_params=params(56),
        cost_estimate=pl.CostEstimate(flops=30000 * MIB, bytes_accessed=0, transcendentals=0),
        name="own_terms",
    )(order, in_hbm(normed), in_hbm(normed), in_hbm(both), in_hbm(after))


def add_kernel(own_ref, got0_ref, got1_ref, after_ref, out_ref):
    def part(got_ref):
        out_ref[...] = (own_ref[...].astype(F32) + got_ref[...].astype(F32)).astype(BF16)

    pl.when(pl.program_id(0) < 2)(lambda: part(got0_ref))
    pl.when(pl.program_id(0) >= 2)(lambda: part(got1_ref))


def add(own, got, after):
    block = lambda place: pl.BlockSpec((2, *own.shape[1:]), lambda g: (place(g), 0, 0))
    return pl.pallas_call(
        add_kernel,
        grid=(4,),
        in_specs=[
            block(lambda g: g),
            block(lambda g: jnp.minimum(g, 1)),
            block(lambda g: jnp.maximum(g - 2, 0)),
            UNREAD,
        ],
        out_specs=block(lambda g: g),
        out_shape=pltpu.HBM(own.shape, BF16),
        compiler_params=params(56),
        cost_estimate=pl.CostEstimate(flops=0, bytes_accessed=0, transcendentals=0),
        name="add",
    )(in_hbm(own), *(in_hbm(g) for g in got), in_hbm(after))


def release(values, after):
    n = len(values)
    return pl.pallas_call(
        lambda *refs: None,
        in_specs=[UNREAD] * (n + 1),
        out_specs=[pl.BlockSpec(memory_space=pltpu.HBM)] * n,
        out_shape=[pltpu.HBM(v.shape, v.dtype) for v in values],
        input_output_aliases={k: k for k in range(n)},
        cost_estimate=pl.CostEstimate(flops=0, bytes_accessed=0, transcendentals=0),
        name="release",
    )(*(in_hbm(v) for v in values), in_hbm(after))


def forward_kernel(
    place_ref, normed_ref, both_ref, inv_ref, cos_ref, sin_ref, *refs
):
    w_refs, (key_ref, value_ref, coef_ref, held_ref, done) = refs[:10], refs[11:]
    feats = key_ref.shape[1]
    zh, core, x_here = place_ref[0], place_ref[1], place_ref[2]
    first_step = pl.program_id(0) == 0
    copies = []
    for p, w_ref in enumerate(w_refs):
        c = lax.rem(core + p % 2, 2)
        if p < 2:
            to = held_ref.at[:, zh, c]
        else:
            to = held_ref.at[lax.rem(x_here + 5 - p // 2, 4), 1 - zh, c]
        copies.append(pltpu.make_async_copy(w_ref, to, done.at[p]))

    @pl.when(first_step)
    def _():
        for copy in copies:
            copy.start()

    pre = None
    for z in range(2):
        for copy in copies[:2] if z == 0 else copies[2:]:
            pl.when(first_step)(copy.wait)
        at = lax.rem(zh + z, 2)
        for x in range(4):
            columns = pl.ds(pl.multiple_of(x * 1024 + at * 512, 512), 512)
            w = held_ref[x, at].reshape(512, 2 * feats)
            term = jnp.dot(normed_ref[:, columns], w, preferred_element_type=F32)
            pre = term if pre is None else pre + term
    key_pre, value_pre = pre[:, :feats], pre[:, feats:]
    key_ref[...] = turn(key_pre, cos_ref[...], sin_ref[...], 1.0).astype(BF16)
    value_ref[...] = value_pre.astype(BF16)
    inner = jnp.sum(
        key_pre * both_ref[:, :feats].astype(F32) + value_pre * both_ref[:, feats:].astype(F32), axis=1, keepdims=True
    )
    inv = inv_ref[...]
    coef_ref[...] = inv * inv * (inner * (1.0 / normed_ref.shape[1]))


def forward(place, normed, both, inv, cosine, sine, weights, after):
    rows, width = normed.shape
    feats = both.shape[1] // 2
    tb = 256
    by_rows = lambda n: pl.BlockSpec((tb, n), lambda i, place: (i, 0))
    return pl.pallas_call(
        forward_kernel,
        grid_spec=pltpu.PrefetchScalarGridSpec(
            num_scalar_prefetch=1,
            grid=(rows // tb,),
            in_specs=[by_rows(width), by_rows(2 * feats), by_rows(HEAD), by_rows(HEAD), by_rows(HEAD)] + [UNREAD] * 11,
            out_specs=[by_rows(feats), by_rows(feats), by_rows(HEAD)],
            scratch_shapes=[pltpu.VMEM((4, 2, 2, 256, 2 * feats), BF16), pltpu.SemaphoreType.DMA((10,))],
        ),
        out_shape=[
            pltpu.HBM((rows, feats), BF16),
            pltpu.HBM((rows, feats), BF16),
            pltpu.HBM((rows, HEAD), F32),
        ],
        compiler_params=params(56),
        cost_estimate=pl.CostEstimate(flops=4 * rows * width * feats, bytes_accessed=20 * MIB, transcendentals=0),
        name="forward",
    )(place, in_hbm(normed), in_hbm(both), in_hbm(inv), cosine, sine, *(in_hbm(w) for w in weights), in_hbm(after))


def backward_kernel(place_ref, tok_ref, both_ref, inv_ref, coef_ref, gain_ref, *refs):
    w_refs, out_ref = refs[:10], refs[10]

    def part(pair):
        for c, w_ref in enumerate(pair):
            s = pl.ds(pl.multiple_of(lax.rem(place_ref[8] + c, 2) * 256, 256), 256)
            w = w_ref[...].reshape(256, both_ref.shape[1])
            grad = lax.dot_general(both_ref[...], w, (((1,), (1,)), ((), ())), preferred_element_type=F32)
            out = inv_ref[:, :1] * (grad * gain_ref[:, s]) - tok_ref[:, s].astype(F32) * coef_ref[:, :1]
            out_ref[:, s] = out.astype(BF16)

    i = pl.program_id(0)
    pl.when(i < 4)(lambda: part(w_refs[:2]))
    for d in range(4):
        pl.when(i == 4 + d)(lambda d=d: part(w_refs[2 + 2 * d : 4 + 2 * d]))


def backward(place, tokens, both, inv, coef, gain, weights):
    rows, width = tokens.shape
    feats = both.shape[1] // 2
    cb = 512
    whole = lambda n: pl.BlockSpec((rows, n), lambda i, place: (0, 0))
    columns = pl.BlockSpec((rows, cb), lambda i, place: (0, place[i]))
    block = pl.BlockSpec((1, 256, 2 * feats), lambda i, place: (jnp.minimum(i, 3), 0, 0))
    return pl.pallas_call(
        backward_kernel,
        grid_spec=pltpu.PrefetchScalarGridSpec(
            num_scalar_prefetch=1,
            grid=(width // cb,),
            in_specs=[
                columns,
                whole(2 * feats),
                whole(HEAD),
                whole(HEAD),
                pl.BlockSpec((1, cb), lambda i, place: (0, place[i])),
                block,
                block,
            ]
            + [pl.BlockSpec((256, 2 * feats), lambda i, place: (0, 0))] * 8,
            out_specs=columns,
        ),
        out_shape=pltpu.HBM((rows, width), BF16),
        compiler_params=params(56),
        cost_estimate=pl.CostEstimate(flops=4 * rows * width * feats, bytes_accessed=28 * MIB, transcendentals=0),
        name="backward",
    )(place, in_hbm(tokens), in_hbm(both), in_hbm(inv), in_hbm(coef), gain, *(in_hbm(w) for w in weights))


def total_kernel(count, got_ref, kw_ref, vw_ref, gain_ref, after_ref, out_ref, gain_out_ref, sum_ref):
    g = pl.program_id(0)
    feats = kw_ref.shape[1]
    part = got_ref[0].astype(F32)
    for j in range(1, got_ref.shape[0]):
        part += got_ref[j].astype(F32)

    @pl.when(g == 0)
    def _():
        sum_ref[...] = part

    @pl.when(g > 0)
    def _():
        sum_ref[...] += part

    @pl.when(g == pl.num_programs(0) - 1)
    def _():
        mean = sum_ref[...] * (1.0 / count)
        out_ref[...] = mean.astype(BF16)
        products = mean[:, :feats] * kw_ref[...].astype(F32) + mean[:, feats:] * vw_ref[...].astype(F32)
        sums = jnp.broadcast_to(jnp.sum(products, axis=1, keepdims=True), (products.shape[0], HEAD)).T
        line = jnp.concatenate([sums[:1]] * (HEAD // sums.shape[1]), axis=1) / gain_ref[...]
        gain_out_ref[...] = jnp.broadcast_to(line, gain_out_ref.shape)


def total(count, copies, got, key_rows, value_rows, gain_rows, after):
    sources, rows, width = got.shape
    feats = key_rows.shape[1]
    fixed = lambda shape: pl.BlockSpec(shape, lambda g: (0,) * len(shape))
    return pl.pallas_call(
        lambda *refs: total_kernel(count, *refs),
        grid=(4,),
        in_specs=[
            pl.BlockSpec((sources // 4, rows, width), lambda g: (g, 0, 0)),
            fixed((rows, feats)),
            fixed((rows, feats)),
            fixed((1, HEAD)),
            UNREAD,
        ],
        out_specs=[fixed((rows, width)), fixed((copies, HEAD))],
        out_shape=[pltpu.HBM((rows, width), BF16), pltpu.HBM((copies, HEAD), F32)],
        scratch_shapes=[pltpu.VMEM((rows, width), F32)],
        compiler_params=params(56),
        cost_estimate=pl.CostEstimate(flops=2 * MIB, bytes_accessed=5 * MIB, transcendentals=0),
        name="total",
    )(in_hbm(got), key_rows, value_rows, gain_rows, in_hbm(after))


def pair_kernel(zl_ref, mine_ref, got_ref, out_ref):
    out_ref[zl_ref[0]] = mine_ref[...]
    out_ref[1 - zl_ref[0]] = got_ref[...]


def pair(zl, mine, got):
    vmem = pl.BlockSpec(memory_space=pltpu.VMEM)
    return pl.pallas_call(
        pair_kernel,
        in_specs=[pl.BlockSpec(memory_space=pltpu.SMEM), vmem, vmem],
        out_specs=vmem,
        out_shape=jax.ShapeDtypeStruct((2, *mine.shape), BF16),
        compiler_params=params(8),
        cost_estimate=pl.CostEstimate(flops=0, bytes_accessed=0, transcendentals=0),
        name="pair",
    )(zl.reshape(1), mine, got)


def finish_kernel(y_ref, p0_ref, p1_ref, p2_ref, p3_ref, key_ref, value_ref):
    feats = key_ref.shape[1]
    for d, p_ref in enumerate((p0_ref, p1_ref, p2_ref, p3_ref)):
        for z in range(2):
            first = lax.rem(y_ref[0] + 4 - d, 4) * 64 + z * 32
            at = pl.ds(pl.multiple_of(first, 32), 32)
            key_ref[at, :] = p_ref[z, :, :feats].astype(F32)
            value_ref[at, :] = p_ref[z, :, feats:].astype(F32)


def finish(y, pieces):
    pairs, rows, width = pieces[0].shape
    vmem = pl.BlockSpec(memory_space=pltpu.VMEM)
    return pl.pallas_call(
        finish_kernel,
        in_specs=[pl.BlockSpec(memory_space=pltpu.SMEM)] + [vmem] * 4,
        out_specs=[vmem] * 2,
        out_shape=[pltpu.HBM((4 * pairs * rows, width // 2), F32)] * 2,
        compiler_params=params(8),
        cost_estimate=pl.CostEstimate(flops=MIB, bytes_accessed=2 * MIB, transcendentals=0),
        name="finish",
    )(y.reshape(1), *pieces)


def shards(tokens, norm_gain, key_weight, value_weight, key_cotangent, value_cotangent):
    length, width = tokens.shape
    feats = key_weight.shape[1]
    count = math.prod(SIZES)
    x, zh, core, y, zl = (lax.axis_index(a).astype(jnp.int32) for a in AXES)
    half = HEAD // 2
    angles = np.arange(length)[:, None] * np.exp(-(2.0 * np.arange(half) / HEAD) * math.log(500000.0))[None, :]
    cosine = jnp.asarray(np.concatenate([np.cos(angles), np.cos(angles)], 1).astype(np.float32))
    sine = jnp.asarray(np.concatenate([-np.sin(angles), np.sin(angles)], 1).astype(np.float32))
    gain = norm_gain.reshape(1, width)

    shard = jnp.concatenate([key_weight, value_weight], axis=1)
    spread = jnp.broadcast_to(shard[None], (4, 256, 2 * feats))
    near = lax.all_to_all(spread, "x", 0, 0, tiled=True)
    far = send(shard, lambda x, y, z, c: (x, y, z + 2, c))
    far = [far] + [send(far, lambda x, y, z, c, d=d: (x + d, y, z, c)) for d in (1, 2, 3)]

    blocks = jnp.arange(8, dtype=jnp.int32) * 2
    both, inv, normed, *sibling = norm_and_terms(
        blocks + 1 - core, tokens, gain, key_cotangent, value_cotangent, cosine, sine, spread
    )
    sibling = [to_core(s) for s in sibling]
    terms = add(own_terms(blocks + core, normed, both, near), sibling, inv)
    terms, near, *far = release([terms, near, *far], inv)
    got = lax.all_to_all(terms.reshape(64, 32, 2 * feats), ("x", "zh", "y", "zl"), 0, 0, tiled=True)

    weights = [near, to_core(near)]
    for w in far:
        weights += [w, to_core(w)]
    rotated_keys, value_rows, coef = forward(
        jnp.stack([zh, core, x]), normed, both, inv, cosine, sine, weights, terms
    )
    i4 = jnp.arange(4, dtype=jnp.int32)
    place = jnp.concatenate([i4 * 2 + zh, (x + 4 - i4) % 4 * 2 + 1 - zh, core.reshape(1)])
    input_grad = backward(place, tokens, both, inv, coef, gain, weights)

    row = (y * 2 + zl) * 32
    key_rows, value_rows_of = (lax.dynamic_slice(w, (row, 0), (32, feats)) for w in (key_weight, value_weight))
    own_gain = lax.dynamic_slice(norm_gain, ((x * 4 + zh * 2 + core) * 256 + row,), (32,))
    mean, gain_rows = total(count, count // 2, got, key_rows, value_rows_of, jnp.tile(own_gain, 4).reshape(1, HEAD), input_grad)
    gain_rows = lax.all_to_all(gain_rows, ("x", "zh", "y", "zl"), 0, 0, tiled=True)
    gain_rows = gain_rows.reshape(4, 2, 8, HEAD)[..., :32]
    gain_other = to_core(gain_rows)
    by_core = lambda mine: jnp.where(core == mine, gain_rows, gain_other)
    gain_grad = jnp.stack([by_core(0), by_core(1)], axis=2).reshape(width)
    pieces = pair(zl, mean, send(mean, lambda x, y, z, c: (x, y, z ^ 1, c)))
    pieces = [pieces] + [send(pieces, lambda x, y, z, c, d=d: (x, y + d, z, c)) for d in (1, 2, 3)]
    key_grad, value_grad = finish(y, pieces)
    return rotated_keys, value_rows, input_grad, key_grad, value_grad, gain_grad


def solution(mesh):
    fine = Mesh(mesh.devices.reshape(SIZES), AXES)
    fsdp, replica = ("x", "zh", "c"), ("y", "zl")
    in_specs = (P(fsdp + replica, None), P(), P(fsdp, None), P(fsdp, None), P(fsdp + replica, None), P(fsdp + replica, None))
    out_specs = (P(fsdp + replica, None), P(fsdp + replica, None), P(fsdp + replica, None), P(fsdp, None), P(fsdp, None), P())
    return jax.shard_map(shards, mesh=fine, in_specs=in_specs, out_specs=out_specs, check_vma=False)
```

```python
import math

import jax
import jax.numpy as jnp
import numpy as np
from jax import lax
from jax.experimental import pallas as pl
from jax.experimental.pallas import tpu as pltpu
from jax.sharding import Mesh, PartitionSpec as P

HEAD = 128
AXES = ("x", "zh", "c", "y", "zl")
SIZES = (4, 2, 2, 4, 2)
F32 = jnp.float32
BF16 = jnp.bfloat16
MIB = 1 << 20


def send(value, move):
    pairs = []
    for i in range(math.prod(SIZES)):
        x, zh, c, y, zl = (int(v) for v in np.unravel_index(i, SIZES))
        x, y, z, c = move(x, y, zh * 2 + zl, c)
        x, y, z, c = x % 4, y % 4, z % 4, c % 2
        pairs.append((i, int(np.ravel_multi_index((x, z // 2, c, y, z % 2), SIZES))))
    return lax.ppermute(value, AXES, pairs)


def to_core(value):
    return send(value, lambda x, y, z, c: (x, y, z, c + 1))


def params(mib, **more):
    return pltpu.CompilerParams(vmem_limit_bytes=mib * MIB, **more)


def turn(values, cosine, sine, direction):
    parts = []
    for h in range(values.shape[1] // HEAD):
        v = values[:, h * HEAD : (h + 1) * HEAD]
        parts.append(v * cosine + direction * (pltpu.roll(v, HEAD // 2, 1) * sine))
    return jnp.concatenate(parts, axis=1)


RESIDENT = pl.BlockSpec(memory_space=pltpu.VMEM)
UNREAD = pl.BlockSpec(memory_space=pl.ANY)


def in_hbm(value):
    return pltpu.with_memory_space_constraint(value, pltpu.HBM)


COLUMNS = (((0,), (0,)), ((), ()))


def norm_kernel(
    order_ref, tok_ref, gain_ref, kc_ref, vc_ref, cos_ref, sin_ref, after_ref,
    both_out_ref, inv_ref, stored_ref, t0_ref, t1_ref, normed_ref, both_ref, done,
):
    i = pl.program_id(0)
    tb, feats = kc_ref.shape
    store = pltpu.make_async_copy(normed_ref, stored_ref, done)

    @pl.when(i < 4)
    def _():
        v = tok_ref[...].astype(F32)
        inv = lax.rsqrt(jnp.mean(v * v, axis=1, keepdims=True) + 1e-05)
        inv_ref[...] = jnp.broadcast_to(inv, inv_ref.shape)
        normed_ref[pl.ds(pl.multiple_of(i * tb, tb), tb), :] = (v * inv * gain_ref[...]).astype(BF16)
        here = pl.ds(pl.multiple_of(i * tb, tb), tb)
        back = turn(kc_ref[...].astype(F32), cos_ref[...], sin_ref[...], -1.0).astype(BF16)
        both_ref[here, :feats] = back
        both_ref[here, feats:] = vc_ref[...]
        both_out_ref[:, :feats] = back
        both_out_ref[:, feats:] = vc_ref[...]

    @pl.when(i == 4)
    def _():
        store.start()

    def part(p, terms_ref):
        for j in range(2):
            columns = pl.ds(pl.multiple_of(order_ref[p * 2 + j] * 256, 256), 256)
            term = lax.dot_general(normed_ref[:, columns], both_ref[...], COLUMNS, preferred_element_type=F32)
            terms_ref[p % 2 * 2 + j] = term.astype(BF16)

    for p in range(4):
        pl.when(i == 4 + p)(lambda p=p: part(p, (t0_ref, t1_ref)[p // 2]))

    @pl.when(i == 7)
    def _():
        store.wait()


def norm_and_terms(order, tokens, gain, key_cot, value_cot, cosine, sine, after):
    rows, width = tokens.shape
    feats = key_cot.shape[1]
    tb = rows // 4
    by_rows = lambda n: pl.BlockSpec((tb, n), lambda i, order: (jnp.minimum(i, 3), 0))
    return pl.pallas_call(
        norm_kernel,
        grid_spec=pltpu.PrefetchScalarGridSpec(
            num_scalar_prefetch=1,
            grid=(8,),
            in_specs=[
                by_rows(width),
                pl.BlockSpec((1, width), lambda i, order: (0, 0)),
                by_rows(feats),
                by_rows(feats),
                by_rows(HEAD),
                by_rows(HEAD),
                UNREAD,
            ],
            out_specs=[
                by_rows(2 * feats),
                by_rows(HEAD),
                pl.BlockSpec(memory_space=pltpu.HBM),
            ]
            + [pl.BlockSpec((4, 256, 2 * feats), lambda i, order: (0, 0, 0))] * 2,
            scratch_shapes=[
                pltpu.VMEM((rows, width), BF16),
                pltpu.VMEM((rows, 2 * feats), BF16),
                pltpu.SemaphoreType.DMA,
            ],
        ),
        out_shape=[
            pltpu.HBM((rows, 2 * feats), BF16),
            pltpu.HBM((rows, HEAD), F32),
            pltpu.HBM((rows, width), BF16),
        ]
        + [pltpu.HBM((4, 256, 2 * feats), BF16)] * 2,
        compiler_params=params(56),
        cost_estimate=pl.CostEstimate(flops=10000 * MIB, bytes_accessed=20 * MIB, transcendentals=0),
        name="norm_and_terms",
    )(order, in_hbm(tokens), gain, in_hbm(key_cot), in_hbm(value_cot), cosine, sine, in_hbm(after))


def own_kernel(order_ref, n0_ref, n1_ref, both_ref, after_ref, terms_ref):
    for j, n_ref in enumerate((n0_ref, n1_ref)):
        term = lax.dot_general(n_ref[...], both_ref[...], COLUMNS, preferred_element_type=F32)
        terms_ref[j] = term.astype(BF16)


def own_terms(order, normed, both, after):
    rows, feats = both.shape
    block = lambda j: pl.BlockSpec((rows, 256), lambda g, order: (0, order[2 * g + j]))
    return pl.pallas_call(
        own_kernel,
        grid_spec=pltpu.PrefetchScalarGridSpec(
            num_scalar_prefetch=1,
            grid=(4,),
            in_specs=[block(0), block(1), pl.BlockSpec((rows, feats), lambda g, order: (0, 0)), UNREAD],
            out_specs=pl.BlockSpec((2, 256, feats), lambda g, order: (g, 0, 0)),
        ),
        out_shape=pltpu.HBM((8, 256, feats), BF16),
        compiler_params=params(56),
        cost_estimate=pl.CostEstimate(flops=30000 * MIB, bytes_accessed=0, transcendentals=0),
        name="own_terms",
    )(order, in_hbm(normed), in_hbm(normed), in_hbm(both), in_hbm(after))


def add_kernel(own_ref, got0_ref, got1_ref, after_ref, out_ref):
    def part(got_ref):
        out_ref[...] = (own_ref[...].astype(F32) + got_ref[...].astype(F32)).astype(BF16)

    pl.when(pl.program_id(0) < 2)(lambda: part(got0_ref))
    pl.when(pl.program_id(0) >= 2)(lambda: part(got1_ref))


def add(own, got, after):
    block = lambda place: pl.BlockSpec((2, *own.shape[1:]), lambda g: (place(g), 0, 0))
    return pl.pallas_call(
        add_kernel,
        grid=(4,),
        in_specs=[
            block(lambda g: g),
            block(lambda g: jnp.minimum(g, 1)),
            block(lambda g: jnp.maximum(g - 2, 0)),
            UNREAD,
        ],
        out_specs=block(lambda g: g),
        out_shape=pltpu.HBM(own.shape, BF16),
        compiler_params=params(56),
        cost_estimate=pl.CostEstimate(flops=0, bytes_accessed=0, transcendentals=0),
        name="add",
    )(in_hbm(own), *(in_hbm(g) for g in got), in_hbm(after))


def release(values, after):
    n = len(values)
    return pl.pallas_call(
        lambda *refs: None,
        in_specs=[UNREAD] * (n + 1),
        out_specs=[pl.BlockSpec(memory_space=pltpu.HBM)] * n,
        out_shape=[pltpu.HBM(v.shape, v.dtype) for v in values],
        input_output_aliases={k: k for k in range(n)},
        cost_estimate=pl.CostEstimate(flops=0, bytes_accessed=0, transcendentals=0),
        name="release",
    )(*(in_hbm(v) for v in values), in_hbm(after))


def forward_kernel(
    place_ref, normed_ref, both_ref, inv_ref, cos_ref, sin_ref, *refs
):
    w_refs, (key_ref, value_ref, coef_ref, held_ref, done) = refs[:10], refs[11:]
    feats = key_ref.shape[1]
    zh, core, x_here = place_ref[0], place_ref[1], place_ref[2]
    first_step = pl.program_id(0) == 0
    copies = []
    for p, w_ref in enumerate(w_refs):
        c = lax.rem(core + p % 2, 2)
        if p < 2:
            to = held_ref.at[:, zh, c]
        else:
            to = held_ref.at[lax.rem(x_here + 5 - p // 2, 4), 1 - zh, c]
        copies.append(pltpu.make_async_copy(w_ref, to, done.at[p]))

    @pl.when(first_step)
    def _():
        for copy in copies:
            copy.start()

    pre = None
    for z in range(2):
        for copy in copies[:2] if z == 0 else copies[2:]:
            pl.when(first_step)(copy.wait)
        at = lax.rem(zh + z, 2)
        for x in range(4):
            columns = pl.ds(pl.multiple_of(x * 1024 + at * 512, 512), 512)
            w = held_ref[x, at].reshape(512, 2 * feats)
            term = jnp.dot(normed_ref[:, columns], w, preferred_element_type=F32)
            pre = term if pre is None else pre + term
    key_pre, value_pre = pre[:, :feats], pre[:, feats:]
    key_ref[...] = turn(key_pre, cos_ref[...], sin_ref[...], 1.0).astype(BF16)
    value_ref[...] = value_pre.astype(BF16)
    inner = jnp.sum(
        key_pre * both_ref[:, :feats].astype(F32) + value_pre * both_ref[:, feats:].astype(F32), axis=1, keepdims=True
    )
    inv = inv_ref[...]
    coef_ref[...] = inv * inv * (inner * (1.0 / normed_ref.shape[1]))


def forward(place, normed, both, inv, cosine, sine, weights, after):
    rows, width = normed.shape
    feats = both.shape[1] // 2
    tb = 256
    by_rows = lambda n: pl.BlockSpec((tb, n), lambda i, place: (i, 0))
    return pl.pallas_call(
        forward_kernel,
        grid_spec=pltpu.PrefetchScalarGridSpec(
            num_scalar_prefetch=1,
            grid=(rows // tb,),
            in_specs=[by_rows(width), by_rows(2 * feats), by_rows(HEAD), by_rows(HEAD), by_rows(HEAD)] + [UNREAD] * 11,
            out_specs=[by_rows(feats), by_rows(feats), by_rows(HEAD)],
            scratch_shapes=[pltpu.VMEM((4, 2, 2, 256, 2 * feats), BF16), pltpu.SemaphoreType.DMA((10,))],
        ),
        out_shape=[
            pltpu.HBM((rows, feats), BF16),
            pltpu.HBM((rows, feats), BF16),
            pltpu.HBM((rows, HEAD), F32),
        ],
        compiler_params=params(56),
        cost_estimate=pl.CostEstimate(flops=4 * rows * width * feats, bytes_accessed=20 * MIB, transcendentals=0),
        name="forward",
    )(place, in_hbm(normed), in_hbm(both), in_hbm(inv), cosine, sine, *(in_hbm(w) for w in weights), in_hbm(after))


def backward_kernel(place_ref, tok_ref, both_ref, inv_ref, coef_ref, gain_ref, *refs):
    w_refs, out_ref = refs[:10], refs[10]

    def part(pair):
        for c, w_ref in enumerate(pair):
            s = pl.ds(pl.multiple_of(lax.rem(place_ref[8] + c, 2) * 256, 256), 256)
            w = w_ref[...].reshape(256, both_ref.shape[1])
            grad = lax.dot_general(both_ref[...], w, (((1,), (1,)), ((), ())), preferred_element_type=F32)
            out = inv_ref[:, :1] * (grad * gain_ref[:, s]) - tok_ref[:, s].astype(F32) * coef_ref[:, :1]
            out_ref[:, s] = out.astype(BF16)

    i = pl.program_id(0)
    pl.when(i < 4)(lambda: part(w_refs[:2]))
    for d in range(4):
        pl.when(i == 4 + d)(lambda d=d: part(w_refs[2 + 2 * d : 4 + 2 * d]))


def backward(place, tokens, both, inv, coef, gain, weights):
    rows, width = tokens.shape
    feats = both.shape[1] // 2
    cb = 512
    whole = lambda n: pl.BlockSpec((rows, n), lambda i, place: (0, 0))
    columns = pl.BlockSpec((rows, cb), lambda i, place: (0, place[i]))
    block = pl.BlockSpec((1, 256, 2 * feats), lambda i, place: (jnp.minimum(i, 3), 0, 0))
    return pl.pallas_call(
        backward_kernel,
        grid_spec=pltpu.PrefetchScalarGridSpec(
            num_scalar_prefetch=1,
            grid=(width // cb,),
            in_specs=[
                columns,
                whole(2 * feats),
                whole(HEAD),
                whole(HEAD),
                pl.BlockSpec((1, cb), lambda i, place: (0, place[i])),
                block,
                block,
            ]
            + [pl.BlockSpec((256, 2 * feats), lambda i, place: (0, 0))] * 8,
            out_specs=columns,
        ),
        out_shape=pltpu.HBM((rows, width), BF16),
        compiler_params=params(56),
        cost_estimate=pl.CostEstimate(flops=4 * rows * width * feats, bytes_accessed=28 * MIB, transcendentals=0),
        name="backward",
    )(place, in_hbm(tokens), in_hbm(both), in_hbm(inv), in_hbm(coef), gain, *(in_hbm(w) for w in weights))


def total_kernel(count, got_ref, kw_ref, vw_ref, gain_ref, after_ref, out_ref, gain_out_ref, sum_ref):
    g = pl.program_id(0)
    feats = kw_ref.shape[1]
    part = got_ref[0].astype(F32)
    for j in range(1, got_ref.shape[0]):
        part += got_ref[j].astype(F32)

    @pl.when(g == 0)
    def _():
        sum_ref[...] = part

    @pl.when(g > 0)
    def _():
        sum_ref[...] += part

    @pl.when(g == pl.num_programs(0) - 1)
    def _():
        mean = sum_ref[...] * (1.0 / count)
        out_ref[...] = mean.astype(BF16)
        products = mean[:, :feats] * kw_ref[...].astype(F32) + mean[:, feats:] * vw_ref[...].astype(F32)
        sums = jnp.broadcast_to(jnp.sum(products, axis=1, keepdims=True), (products.shape[0], HEAD)).T
        line = jnp.concatenate([sums[:1]] * (HEAD // sums.shape[1]), axis=1) / gain_ref[...]
        gain_out_ref[...] = jnp.broadcast_to(line, gain_out_ref.shape)


def total(count, copies, got, key_rows, value_rows, gain_rows, after):
    sources, rows, width = got.shape
    feats = key_rows.shape[1]
    fixed = lambda shape: pl.BlockSpec(shape, lambda g: (0,) * len(shape))
    return pl.pallas_call(
        lambda *refs: total_kernel(count, *refs),
        grid=(4,),
        in_specs=[
            pl.BlockSpec((sources // 4, rows, width), lambda g: (g, 0, 0)),
            fixed((rows, feats)),
            fixed((rows, feats)),
            fixed((1, HEAD)),
            UNREAD,
        ],
        out_specs=[fixed((rows, width)), fixed((copies, HEAD))],
        out_shape=[pltpu.HBM((rows, width), BF16), pltpu.HBM((copies, HEAD), F32)],
        scratch_shapes=[pltpu.VMEM((rows, width), F32)],
        compiler_params=params(56),
        cost_estimate=pl.CostEstimate(flops=2 * MIB, bytes_accessed=5 * MIB, transcendentals=0),
        name="total",
    )(in_hbm(got), key_rows, value_rows, gain_rows, in_hbm(after))


def pair_kernel(zl_ref, mine_ref, got_ref, out_ref):
    out_ref[zl_ref[0]] = mine_ref[...]
    out_ref[1 - zl_ref[0]] = got_ref[...]


def pair(zl, mine, got):
    vmem = pl.BlockSpec(memory_space=pltpu.VMEM)
    return pl.pallas_call(
        pair_kernel,
        in_specs=[pl.BlockSpec(memory_space=pltpu.SMEM), vmem, vmem],
        out_specs=vmem,
        out_shape=jax.ShapeDtypeStruct((2, *mine.shape), BF16),
        compiler_params=params(8),
        cost_estimate=pl.CostEstimate(flops=0, bytes_accessed=0, transcendentals=0),
        name="pair",
    )(zl.reshape(1), mine, got)


def finish_kernel(y_ref, p0_ref, p1_ref, p2_ref, p3_ref, key_ref, value_ref):
    feats = key_ref.shape[1]
    for d, p_ref in enumerate((p0_ref, p1_ref, p2_ref, p3_ref)):
        for z in range(2):
            first = lax.rem(y_ref[0] + 4 - d, 4) * 64 + z * 32
            at = pl.ds(pl.multiple_of(first, 32), 32)
            key_ref[at, :] = p_ref[z, :, :feats].astype(F32)
            value_ref[at, :] = p_ref[z, :, feats:].astype(F32)


def finish(y, pieces):
    pairs, rows, width = pieces[0].shape
    vmem = pl.BlockSpec(memory_space=pltpu.VMEM)
    return pl.pallas_call(
        finish_kernel,
        in_specs=[pl.BlockSpec(memory_space=pltpu.SMEM)] + [vmem] * 4,
        out_specs=[vmem] * 2,
        out_shape=[pltpu.HBM((4 * pairs * rows, width // 2), F32)] * 2,
        compiler_params=params(8),
        cost_estimate=pl.CostEstimate(flops=MIB, bytes_accessed=2 * MIB, transcendentals=0),
        name="finish",
    )(y.reshape(1), *pieces)


def shards(tokens, norm_gain, key_weight, value_weight, key_cotangent, value_cotangent):
    length, width = tokens.shape
    feats = key_weight.shape[1]
    count = math.prod(SIZES)
    x, zh, core, y, zl = (lax.axis_index(a).astype(jnp.int32) for a in AXES)
    half = HEAD // 2
    angles = np.arange(length)[:, None] * np.exp(-(2.0 * np.arange(half) / HEAD) * math.log(500000.0))[None, :]
    cosine = jnp.asarray(np.concatenate([np.cos(angles), np.cos(angles)], 1).astype(np.float32))
    sine = jnp.asarray(np.concatenate([-np.sin(angles), np.sin(angles)], 1).astype(np.float32))
    gain = norm_gain.reshape(1, width)

    shard = jnp.concatenate([key_weight, value_weight], axis=1)
    spread = jnp.broadcast_to(shard[None], (4, 256, 2 * feats))
    near = lax.all_to_all(spread, "x", 0, 0, tiled=True)
    far = send(shard, lambda x, y, z, c: (x, y, z + 2, c))
    far = [far] + [send(far, lambda x, y, z, c, d=d: (x + d, y, z, c)) for d in (1, 2, 3)]

    blocks = jnp.arange(8, dtype=jnp.int32) * 2
    both, inv, normed, *sibling = norm_and_terms(
        blocks + 1 - core, tokens, gain, key_cotangent, value_cotangent, cosine, sine, spread
    )
    sibling = [to_core(s) for s in sibling]
    terms = add(own_terms(blocks + core, normed, both, near), sibling, inv)
    near, *far = release([near, *far], terms)
    got = lax.all_to_all(terms.reshape(64, 32, 2 * feats), ("x", "zh", "y", "zl"), 0, 0, tiled=True)

    weights = [near, to_core(near)]
    for w in far:
        weights += [w, to_core(w)]
    rotated_keys, value_rows, coef = forward(
        jnp.stack([zh, core, x]), normed, both, inv, cosine, sine, weights, terms
    )
    i4 = jnp.arange(4, dtype=jnp.int32)
    place = jnp.concatenate([i4 * 2 + zh, (x + 4 - i4) % 4 * 2 + 1 - zh, core.reshape(1)])
    input_grad = backward(place, tokens, both, inv, coef, gain, weights)

    row = (y * 2 + zl) * 32
    key_rows, value_rows_of = (lax.dynamic_slice(w, (row, 0), (32, feats)) for w in (key_weight, value_weight))
    own_gain = lax.dynamic_slice(norm_gain, ((x * 4 + zh * 2 + core) * 256 + row,), (32,))
    mean, gain_rows = total(count, count // 2, got, key_rows, value_rows_of, jnp.tile(own_gain, 4).reshape(1, HEAD), input_grad)
    gain_rows = lax.all_to_all(gain_rows, ("x", "zh", "y", "zl"), 0, 0, tiled=True)
    gain_rows = gain_rows.reshape(4, 2, 8, HEAD)[..., :32]
    gain_other = to_core(gain_rows)
    by_core = lambda mine: jnp.where(core == mine, gain_rows, gain_other)
    gain_grad = jnp.stack([by_core(0), by_core(1)], axis=2).reshape(width)
    pieces = pair(zl, mean, send(mean, lambda x, y, z, c: (x, y, z ^ 1, c)))
    pieces = [pieces] + [send(pieces, lambda x, y, z, c, d=d: (x, y + d, z, c)) for d in (1, 2, 3)]
    key_grad, value_grad = finish(y, pieces)
    return rotated_keys, value_rows, input_grad, key_grad, value_grad, gain_grad


def solution(mesh):
    fine = Mesh(mesh.devices.reshape(SIZES), AXES)
    fsdp, replica = ("x", "zh", "c"), ("y", "zl")
    in_specs = (P(fsdp + replica, None), P(), P(fsdp, None), P(fsdp, None), P(fsdp + replica, None), P(fsdp + replica, None))
    out_specs = (P(fsdp + replica, None), P(fsdp + replica, None), P(fsdp + replica, None), P(fsdp, None), P(fsdp, None), P())
    return jax.shard_map(shards, mesh=fine, in_specs=in_specs, out_specs=out_specs, check_vma=False)
```
